128 devices in a mesh: lon: 32 (over z, x, core), lat: 4 (over y).
Axes of the slice: x: 4, y: 4, z: 4, core: 2. Of those that a mesh axis runs over, the one named last changes fastest.
Arguments:
- obs_values: bfloat16 [16384, 1, 128, 128], P(('lon', 'lat')), may hold values from -6 to 6
- obs_weights: float32 [16384, 1, 128], P(('lon', 'lat')), may hold values from 0.3 to 3
- block_counts: int32 [16384, 1], P(('lon', 'lat')), may hold values from 0 to 128, as said below
- obs_cells: int32 [16384, 1, 128], P(('lon', 'lat')), may hold values from 0 to 127
- block_tiles: int32 [16384, 1], P(('lon', 'lat')), may hold values from 0 to 95
- shift_offsets: int32 [2], replicated, may hold values from 1 to 7
- embed_weight: bfloat16 [128, 128], replicated, may hold values from -0.5 to 0.5
- patch_weight: bfloat16 [2048, 1024], replicated, may hold values from -0.125 to 0.125
- norm_gain: float32 [1024], replicated, may hold values from 0.25 to 1.75
- qkv_weight: bfloat16 [1024, 3072], replicated, as said below
- proj_weight: bfloat16 [1024, 1024], replicated, may hold values from -0.1875 to 0.1875
- out_gain: float32 [1024], replicated, may hold values from 0.25 to 1.75
- unembed_weight: bfloat16 [1024, 2048], replicated, may hold values from -0.1875 to 0.1875
- read_weight: bfloat16 [128, 128], replicated, may hold values from -0.5 to 0.5
Outputs:
- obs_pred: bfloat16 [16384, 1, 128, 128], P(('lon', 'lat'))
The draws below stay inside these ranges and needn't reach their ends.
Inputs may be any that keep to these rules, and one draw needn't show every extreme that they name: Only the first block_counts[b] slots of block b hold observations; the others are padding. `qkv_weight`: Query, key and value columns in that order, each head's 32 columns together.
All inputs are finite; a program needn't handle non-finite values.
Results may differ from the reference program's by a relative error of at most 0.014.
Values may be sent and summed in bfloat16 or wider, within the bound.
No kernel may reach another device: no remote copies, remote signals or barrier semaphores. Data moves between devices by JAX's collectives and lax.ppermute only.
A program may use at most 192 MiB of HBM per device.

```python
import math
import jax
import jax.numpy as jnp
from jax import lax

FEAT = 128
CH = 128
D = 1024
HEADS = 32
PATCH = 4
WIN = 8
TPATCH = 8
TILE = 128
BLK = 128
CAP = 1
HP = 32
WP = 24
TILE_DEV = 96
PH = 128
PW = 768
N_LON = 32
N_LAT = 4
DEVICES = 128


def draw_block_counts(key, part):
    key = jax.random.fold_in(key, 11)
    first_key, second_key = jax.random.split(key)
    devices = N_LON * N_LAT
    drawn_counts = jax.random.randint(first_key, (devices, devices, CAP), 0, BLK + 1)
    levels = jax.random.randint(second_key, (1, devices, 1), 1, 5)
    counts = jnp.minimum(BLK, drawn_counts * levels // 2).reshape(devices * devices, CAP)
    counts = counts.at[0, 0].set(BLK).at[1, 0].set(0)
    return counts.astype(jnp.int32)


def draw_qkv_weight(key, part):
    key = jax.random.fold_in(key, 23)
    first_key = jax.random.fold_in(key, 0)
    initial = jax.random.normal(first_key, (D, 3 * D), jnp.float32) / math.sqrt(D)
    return initial.astype(jnp.bfloat16)


def place_ends(drawn, rng, smallest, top_value):
    longest = drawn.shape.index(max(drawn.shape))
    spots = []
    for shift in (0, 1):
        where = [jax.random.randint(jax.random.fold_in(rng, axis), (), 0, length) for axis, length in enumerate(drawn.shape)]
        where[longest] = (where[longest] + shift) % drawn.shape[longest]
        spots.append(tuple(where))
    return drawn.at[spots[0]].set(smallest).at[spots[1]].set(top_value)


def shard_levels(rng, dims, cuts, least, top_value):
    loudness, own = 1.0, jax.random.fold_in(rng, 6)
    for axis_at, blocks in cuts:
        heights = jnp.exp(jax.random.uniform(jax.random.fold_in(own, axis_at), (blocks,), jnp.float32, least / len(cuts), top_value / len(cuts)))
        loudness = loudness * jnp.repeat(heights, dims[axis_at] // blocks).reshape([-1 if axis == axis_at else 1 for axis in range(len(dims))])
    return loudness


def normal_values(key, shape, width, limit, cuts=(), kind=jnp.bfloat16):
    gain = shard_levels(key, shape, cuts, -0.22, 0.18) if cuts else 1.0
    result = jax.random.normal(key, shape, jnp.float32) * width * gain
    return jnp.minimum(jnp.maximum(result, -limit), limit).astype(kind)


def setup_inputs(seed: int = 0) -> dict:
    keys = jax.random.split(jax.random.key(seed), 15)
    obs_values = normal_values(keys[0], (DEVICES * DEVICES, CAP, BLK, FEAT), 1.0, 6.0, ((0, 128),))
    obs_weights = jnp.clip(jnp.exp(math.log(3.0) - 2.3025851 * jax.random.uniform(keys[1], (DEVICES * DEVICES, CAP, BLK), jnp.float32) ** shard_levels(keys[1], (DEVICES * DEVICES, CAP, BLK), ((0, 128),), -0.2, 0.2)), 0.3, 3.0)
    block_counts = draw_block_counts(jax.random.fold_in(keys[14], 71), 0)
    obs_cells = place_ends(jax.random.randint(keys[3], (DEVICES * DEVICES, CAP, BLK), 0, TILE), jax.random.fold_in(keys[3], 1), 0, TILE - 1).astype(jnp.int32)
    block_tiles = place_ends(jax.random.randint(keys[4], (DEVICES * DEVICES, CAP), 0, TILE_DEV), jax.random.fold_in(keys[4], 1), 0, TILE_DEV - 1).astype(jnp.int32)
    shift_offsets = jax.random.randint(keys[5], (2,), 1, WIN).astype(jnp.int32)
    embed_weight = normal_values(keys[6], (FEAT, CH), FEAT ** -0.5, 0.5)
    patch_weight = normal_values(keys[7], (PATCH * PATCH * CH, D), (PATCH * PATCH * CH) ** -0.5, 0.125)
    norm_gain = jnp.clip(1.0 + 0.15 * jax.random.normal(keys[8], (D,), jnp.float32), 0.25, 1.75)
    qkv_weight = draw_qkv_weight(jax.random.fold_in(keys[14], 71), 0)
    proj_weight = normal_values(keys[10], (D, D), D ** -0.5, 0.1875)
    out_gain = jnp.clip(1.0 + 0.15 * jax.random.normal(keys[11], (D,), jnp.float32), 0.25, 1.75)
    unembed_weight = normal_values(keys[12], (D, PATCH * PATCH * CH), D ** -0.5, 0.1875)
    read_weight = normal_values(keys[13], (CH, FEAT), CH ** -0.5, 0.5)
    return {"obs_values": obs_values, "obs_weights": obs_weights, "block_counts": block_counts, "obs_cells": obs_cells, "block_tiles": block_tiles, "shift_offsets": shift_offsets, "embed_weight": embed_weight, "patch_weight": patch_weight, "norm_gain": norm_gain, "qkv_weight": qkv_weight, "proj_weight": proj_weight, "out_gain": out_gain, "unembed_weight": unembed_weight, "read_weight": read_weight}


def layer_norm(values, gain_vector):
    row_mean = lax.optimization_barrier(jnp.mean(values, axis=-1, keepdims=True))
    centered = values - row_mean
    variance = lax.optimization_barrier(jnp.mean(centered * centered, axis=-1, keepdims=True))
    return centered * lax.rsqrt(variance + 1e-05) * gain_vector

def window_attention(projected, token_flags):
    head_size = projected.shape[-1]
    queries = projected[:, :, 0].astype(jnp.float32)
    key_rows = projected[:, :, 1].astype(jnp.float32)
    value_rows = projected[:, :, 2].astype(jnp.float32)
    scores = jnp.einsum('nqhd,nkhd->nhqk', queries, key_rows) * head_size ** (-0.5)
    same_region = token_flags[:, None, :, None] == token_flags[:, None, None, :]
    scores = jnp.where(same_region, scores, -1000000000.0)
    row_max = lax.optimization_barrier(jnp.max(scores, axis=-1, keepdims=True))
    expo = jnp.exp(scores - row_max)
    softmax_weights = (expo / lax.optimization_barrier(jnp.sum(expo, axis=-1, keepdims=True))).astype(jnp.bfloat16)
    mixed_out = jnp.einsum('nhqk,nkhd->nqhd', softmax_weights.astype(jnp.float32), value_rows)
    return mixed_out.astype(jnp.bfloat16)

def reference(obs_values, obs_weights, block_counts, obs_cells, block_tiles, shift_offsets, embed_weight, patch_weight, norm_gain, qkv_weight, proj_weight, out_gain, unembed_weight, read_weight):
    devices = N_LON * N_LAT
    tiles_across = WP // TPATCH
    cell_total = PH * PW * PATCH * PATCH
    dest_ids = jnp.arange(devices, dtype=jnp.int32)
    lat_ids = (dest_ids % N_LAT)[:, None, None]
    lon_ids = (dest_ids // N_LAT)[:, None, None]
    tiles_dest = block_tiles.reshape(devices, devices, CAP)
    row_global = lat_ids * HP + tiles_dest // tiles_across
    col_global = lon_ids * tiles_across + tiles_dest % tiles_across
    global_tile = row_global * (PW // TPATCH) + col_global
    cell_ids = (global_tile[..., None] * TILE + obs_cells.reshape(devices, devices, CAP, BLK)).transpose(1, 0, 2, 3)
    values_src = obs_values.reshape(devices, devices, CAP, BLK, FEAT)
    weights_src = obs_weights.reshape(devices, devices, CAP, BLK)
    counts_src = block_counts.reshape(devices, devices, CAP)

    def live_of(counts):
        slots = jnp.arange(BLK, dtype=jnp.int32)[None, None, :]
        return (slots < counts[:, :, None]).astype(jnp.float32)

    def grid_step(grid_sum, pieces):
        values, weights, counts, cells = pieces
        embedded = jax.nn.gelu(jnp.dot(values.reshape(-1, FEAT), embed_weight, preferred_element_type=jnp.float32))
        outgoing = (embedded.reshape(devices, CAP, BLK, CH) * (weights * live_of(counts))[..., None]).astype(jnp.bfloat16)
        grid_sum = grid_sum.at[cells.reshape(-1)].add(outgoing.reshape(-1, CH).astype(jnp.float32))
        return (grid_sum, None)
    grid_sum, _ = lax.scan(grid_step, jnp.zeros((cell_total, CH), jnp.float32), (values_src, weights_src, counts_src, cell_ids))
    patches = grid_sum.astype(jnp.bfloat16).reshape(PH * PW, PATCH * PATCH * CH)
    tokens = jnp.dot(patches, patch_weight, preferred_element_type=jnp.float32).astype(jnp.bfloat16).reshape(PH, PW, D)
    row_shift = shift_offsets[0]
    col_shift = shift_offsets[1]
    rolled = jnp.roll(tokens, (-row_shift, -col_shift), axis=(0, 1))
    normed = layer_norm(rolled.astype(jnp.float32), norm_gain).astype(jnp.bfloat16)

    def row_attention(row_block):
        rows = lax.dynamic_slice_in_dim(normed, row_block * WIN, WIN, 0)
        projected = jnp.dot(rows.reshape(-1, D), qkv_weight, preferred_element_type=jnp.float32).astype(jnp.bfloat16)
        projected = projected.reshape(WIN, PW // WIN, WIN, 3, HEADS, D // HEADS).transpose(1, 0, 2, 3, 4, 5)
        projected = projected.reshape(PW // WIN, WIN * WIN, 3, HEADS, D // HEADS)
        global_rows = row_block * WIN + jnp.arange(WIN, dtype=jnp.int32)
        row_flags = global_rows >= PH - row_shift
        token_flags = jnp.broadcast_to(row_flags[None, :, None], (PW // WIN, WIN, WIN)).reshape(PW // WIN, WIN * WIN)
        attended = window_attention(projected, token_flags)
        return attended.reshape(PW // WIN, WIN, WIN, D).transpose(1, 0, 2, 3).reshape(WIN, PW, D)
    mixed = lax.map(row_attention, jnp.arange(PH // WIN, dtype=jnp.int32)).reshape(PH, PW, D)
    mixed = jnp.roll(mixed, (row_shift, col_shift), axis=(0, 1))
    updated = (tokens.astype(jnp.float32) + jnp.dot(mixed.reshape(-1, D), proj_weight, preferred_element_type=jnp.float32).reshape(PH, PW, D)).astype(jnp.bfloat16)
    normed_out = layer_norm(updated.astype(jnp.float32), out_gain).astype(jnp.bfloat16)
    decoded = jnp.dot(normed_out.reshape(-1, D), unembed_weight, preferred_element_type=jnp.float32).astype(jnp.bfloat16)
    decoded = decoded.reshape(cell_total, CH)

    def read_step(carry, pieces):
        counts, cells = pieces
        sampled = decoded[cells.reshape(-1)]
        predicted = jnp.dot(sampled, read_weight, preferred_element_type=jnp.float32).reshape(devices, CAP, BLK, FEAT)
        return (carry, (predicted * live_of(counts)[..., None]).astype(jnp.bfloat16))
    _, obs_pred = lax.scan(read_step, jnp.zeros((), jnp.float32), (counts_src, cell_ids))
    return obs_pred.reshape(devices * devices, CAP, BLK, FEAT)
```

```python
import jax
import jax.numpy as jnp
from jax import lax
from jax.experimental import pallas as pl
from jax.experimental.pallas import tpu as pltpu
from jax.sharding import PartitionSpec as P

CH = 128
D = 1024
HEADS = 32
HEAD = 32
CELLS = 16
WIN = 8
TILE = 128
HP = 32
WP = 24
TILES = 96
TOKENS = HP * WP
BLOCKS = 128
GROUP = 16
SPAN_R = HP + WIN
SPAN_C = WP + WIN
REGION = SPAN_R * SPAN_C
EXT_R = HP + 2 * WIN
EXT_C = WP + 2 * WIN
WIN_TOK = WIN * WIN
LANES = 128
COLS = 256
DEAD = 1e30
DEAD_LIMIT = 1e6
VMEM_LIMIT = 60 * 1024 * 1024
F32 = jnp.float32
BF16 = jnp.bfloat16


def layer_norm(values, gain_vector):
    row_mean = jnp.mean(values, axis=-1, keepdims=True)
    centered = values - row_mean
    variance = jnp.mean(centered * centered, axis=-1, keepdims=True)
    return centered * lax.rsqrt(variance + 1e-05) * gain_vector


def grid_kernel(
    tiles_ref, cells_ref, received_ref, patch_hbm,
    tokens_ref, west_ref, east_ref, north_ref, south_ref, nw_ref, ne_ref, sw_ref, se_ref, live_cells_ref,
    cell_sums, patch_rows, patch_weight, weight_sem,
):
    step = pl.program_id(0)
    weight_copy = pltpu.make_async_copy(patch_hbm, patch_weight, weight_sem)

    @pl.when(step == 0)
    def _():
        weight_copy.start()

        @pl.loop(0, TILES)
        def _(tile):
            cell_sums[tile] = jnp.zeros((TILE, CH), F32)

    cell_iota = lax.broadcasted_iota(jnp.int32, (TILE, BLOCKS), 0)
    slot_iota = lax.broadcasted_iota(jnp.int32, (1, TILE), 1).astype(F32)
    for b in range(GROUP):
        cells = cells_ref[b : b + 1, :]
        cells = (cells & 15) * 8 + (cells >> 4)
        block = received_ref[b]
        live = block < jnp.asarray(DEAD_LIMIT, BF16)
        block = jnp.where(live, block, jnp.zeros_like(block))
        count = jnp.sum(jnp.where(live, 1.0, 0.0).astype(F32), axis=0, keepdims=True)
        live_cells_ref[b : b + 1, :] = jnp.where(slot_iota < count, cells, -1)
        one_hot = jnp.where(cell_iota == cells, 1.0, 0.0).astype(BF16)
        tile = tiles_ref[step * GROUP + b]
        cell_sums[tile] += jnp.dot(one_hot, block, preferred_element_type=F32)

    @pl.when(step == BLOCKS // GROUP - 1)
    def _():
        @pl.loop(0, TILES // 12)
        def _(part):
            tiles = cell_sums[pl.ds(part * 12, 12)].reshape(12, CELLS, 8, CH)
            for cell in range(CELLS):
                rows = tiles[:, cell].reshape(96, CH).astype(BF16)
                patch_rows[pl.ds(pl.multiple_of(part * 96, 96), 96), cell * CH : (cell + 1) * CH] = rows

        weight_copy.wait()

        @pl.loop(0, 3)
        def _(m):
            @pl.loop(0, D // COLS)
            def _(n):
                rows = pl.ds(pl.multiple_of(m * 256, 256), 256)
                cols = pl.ds(pl.multiple_of(n * COLS, COLS), COLS)
                part = jnp.dot(patch_rows[rows, :], patch_weight[:, cols], preferred_element_type=F32)
                tokens_ref[rows, cols] = part.astype(BF16).astype(F32)

        def edge(row, col):
            first = tokens_ref[pl.ds(pl.multiple_of(row * WP + col, 8), WIN), :]
            second = tokens_ref[pl.ds(pl.multiple_of((row + 1) * WP + col, 8), WIN), :]
            return jnp.concatenate([first, second], axis=0).astype(BF16)

        @pl.loop(0, HP // 2)
        def _(pair):
            rows = pl.ds(pl.multiple_of(pair * 16, 16), 16)
            west_ref[rows, :] = edge(pair * 2, 0)
            east_ref[rows, :] = edge(pair * 2, WP - WIN)

        north_ref[...] = tokens_ref[0 : WIN * WP, :].astype(BF16)
        south_ref[...] = tokens_ref[TOKENS - WIN * WP :, :].astype(BF16)
        nw_ref[...] = west_ref[0:WIN_TOK, :]
        sw_ref[...] = west_ref[HP * WIN - WIN_TOK :, :]
        ne_ref[...] = east_ref[0:WIN_TOK, :]
        se_ref[...] = east_ref[HP * WIN - WIN_TOK :, :]


def grid_tokens(block_tiles, obs_cells, received, patch_weight):
    whole = lambda rows, dtype: (
        jax.ShapeDtypeStruct((rows, D), dtype),
        pl.BlockSpec((rows, D), lambda i, *_: (0, 0)),
    )
    outs = [whole(TOKENS, F32)] + [whole(n, BF16) for n in (256, 256, 192, 192, 64, 64, 64, 64)]
    outs.append(
        (
            jax.ShapeDtypeStruct((BLOCKS, TILE), jnp.int32),
            pl.BlockSpec((GROUP, TILE), lambda i, *_: (i, 0)),
        )
    )
    return pl.pallas_call(
        grid_kernel,
        grid_spec=pltpu.PrefetchScalarGridSpec(
            num_scalar_prefetch=1,
            grid=(BLOCKS // GROUP,),
            in_specs=[
                pl.BlockSpec((GROUP, TILE), lambda i, *_: (i, 0)),
                pl.BlockSpec((GROUP, TILE, CH), lambda i, *_: (i, 0, 0)),
                pl.BlockSpec(memory_space=pl.ANY),
            ],
            out_specs=[spec for _, spec in outs],
            scratch_shapes=[
                pltpu.VMEM((TILES, TILE, CH), F32),
                pltpu.VMEM((TOKENS, CELLS * CH), BF16),
                pltpu.VMEM((CELLS * CH, D), BF16),
                pltpu.SemaphoreType.DMA,
            ],
        ),
        out_shape=[shape for shape, _ in outs],
        compiler_params=pltpu.CompilerParams(
            vmem_limit_bytes=VMEM_LIMIT, dimension_semantics=("arbitrary",)
        ),
        cost_estimate=pl.CostEstimate(flops=4 * 10**9, bytes_accessed=16 * 10**6, transcendentals=0),
        name="grid_tokens",
    )(block_tiles, obs_cells, received, patch_weight)


def attention_group(qkv, mixed, bias, ones, win_row, win_col, group):
    rows = pl.ds(pl.multiple_of((win_row * 4 + win_col) * WIN_TOK, WIN_TOK), WIN_TOK)
    lanes = lambda part: pl.ds(pl.multiple_of(part * D + group * LANES, LANES), LANES)
    query, key, value = (qkv[rows, lanes(part)] for part in range(3))
    head_of_lane = lax.broadcasted_iota(jnp.int32, (WIN_TOK, LANES), 1) // HEAD
    zero = jnp.zeros((WIN_TOK, LANES), BF16)
    spread = lambda x: jnp.concatenate([jnp.where(head_of_lane == h, x, zero) for h in range(4)], axis=0)
    scores = lax.dot_general(
        query, spread(key), (((1,), (1,)), ((), ())), preferred_element_type=F32
    ) * HEAD ** (-0.5)
    low = lax.broadcasted_iota(jnp.int32, (WIN_TOK, LANES), 1) < WIN_TOK
    parts = []
    for half in range(2):
        part = scores[:, half * LANES : (half + 1) * LANES]
        part = jnp.where(bias[...] < 0.5, part, -1000000000.0)
        low_max = jnp.max(jnp.where(low, part, -jnp.inf), axis=-1, keepdims=True)
        high_max = jnp.max(jnp.where(low, -jnp.inf, part), axis=-1, keepdims=True)
        parts.append(jnp.exp(part - jnp.where(low, low_max, high_max)).astype(BF16))
    weights = jnp.concatenate(parts, axis=1)
    both = jnp.dot(weights, jnp.concatenate([spread(value), ones[...]], axis=1), preferred_element_type=F32)
    result = (both[:, :LANES] / both[:, LANES:]).astype(BF16).astype(F32)
    cols = pl.ds(pl.multiple_of(group * LANES, LANES), LANES)
    for i in range(WIN):
        row = (win_row * WIN + i) * SPAN_C + win_col * WIN
        mixed[pl.ds(pl.multiple_of(row, 8), WIN), cols] = result[i * WIN : (i + 1) * WIN]


def tail_kernel(
    meta_ref, tiles_ref, cells_ref, tokens_hbm,
    west_ref, east_ref, north_ref, south_ref, nw_ref, ne_ref, sw_ref, se_ref,
    norm_gain_ref, out_gain_ref, read_ref, qkv_hbm, proj_hbm, unembed_hbm,
    out_hbm,
    ext, mixed, normed, qkv, row_stage, decoded, out_stage, bias, ones, read_pair,
    qkv_weight, proj_weight, unembed_weight, in_sems, out_sems,
):
    row_shift = meta_ref[0]
    col_shift = meta_ref[1]
    special = meta_ref[2]
    copies = [
        pltpu.make_async_copy(tokens_hbm, ext.at[pl.ds(WIN, HP), pl.ds(WIN, WP), :], in_sems.at[0]),
        pltpu.make_async_copy(qkv_hbm, qkv_weight, in_sems.at[1]),
        pltpu.make_async_copy(proj_hbm, proj_weight, in_sems.at[2]),
        pltpu.make_async_copy(unembed_hbm, unembed_weight, in_sems.at[3]),
    ]
    for copy in copies:
        copy.start()

    def place(source, rows, row, col, per_row):
        if per_row == WIN:
            @pl.loop(0, rows // 2)
            def _(pair):
                both = source[pl.ds(pl.multiple_of(pair * 16, 16), 16), :].astype(F32)
                ext[row + pair * 2, col : col + WIN, :] = both[:WIN]
                ext[row + pair * 2 + 1, col : col + WIN, :] = both[WIN:]
        else:
            @pl.loop(0, rows // 2)
            def _(pair):
                both = source[pl.ds(pl.multiple_of(pair * 2 * WP, 2 * WP), 2 * WP), :].astype(F32)
                ext[row + pair * 2, col : col + WP, :] = both[:WP]
                ext[row + pair * 2 + 1, col : col + WP, :] = both[WP:]

    place(west_ref, HP, WIN, 0, WIN)
    place(east_ref, HP, WIN, WIN + WP, WIN)
    place(north_ref, WIN, 0, WIN, WP)
    place(south_ref, WIN, WIN + HP, WIN, WP)
    place(nw_ref, WIN, 0, 0, WIN)
    place(ne_ref, WIN, 0, WIN + WP, WIN)
    place(sw_ref, WIN, WIN + HP, 0, WIN)
    place(se_ref, WIN, WIN + HP, WIN + WP, WIN)

    ones[...] = (
        lax.broadcasted_iota(jnp.int32, (4 * WIN_TOK, LANES), 0) // WIN_TOK
        == lax.broadcasted_iota(jnp.int32, (4 * WIN_TOK, LANES), 1) // HEAD
    ).astype(F32).astype(BF16)
    read_pair[...] = jnp.zeros((2 * CH, 2 * CH), BF16)
    read_pair[:CH, :CH] = read_ref[...]
    read_pair[CH:, CH:] = read_ref[...]
    copies[0].wait()

    @pl.loop(0, SPAN_R)
    def _(r):
        values = layer_norm(ext[row_shift + r], norm_gain_ref[...])
        row_stage[0:SPAN_C, :] = pltpu.roll(values, EXT_C - col_shift, 0)[:SPAN_C]
        win_row = r // WIN
        for win_col in range(4):
            row = (win_row * 4 + win_col) * WIN_TOK + (r % WIN) * WIN
            mixed[pl.ds(pl.multiple_of(row, 8), WIN), :] = row_stage[win_col * WIN : (win_col + 1) * WIN, :]

    @pl.loop(0, REGION // 256)
    def _(m):
        rows = pl.ds(pl.multiple_of(m * 256, 256), 256)
        normed[rows, :] = mixed[rows, :].astype(BF16)

    copies[1].wait()

    @pl.loop(0, 3 * D // COLS)
    def _(n):
        cols = pl.ds(pl.multiple_of(n * COLS, COLS), COLS)

        @pl.loop(0, REGION // 256)
        def _(m):
            rows = pl.ds(pl.multiple_of(m * 256, 256), 256)
            qkv[rows, cols] = jnp.dot(
                normed[rows, :], qkv_weight[:, cols], preferred_element_type=F32
            ).astype(BF16)

    @pl.loop(0, WIN_TOK // WIN)
    def _(i):
        query_flag = jnp.where(i >= WIN - row_shift, 1, 0)
        key_row = (lax.broadcasted_iota(jnp.int32, (WIN, LANES), 1) % WIN_TOK) // WIN
        key_flag = jnp.where(key_row >= WIN - row_shift, 1, 0)
        bias[1, pl.ds(pl.multiple_of(i * WIN, 8), WIN), :] = jnp.where(key_flag == query_flag, 0.0, 1.0)

    bias[0] = jnp.zeros((WIN_TOK, LANES), F32)

    @pl.loop(0, 5)
    def _(win_row):
        which = jnp.where(win_row == special, 1, 0)

        @pl.loop(0, D // LANES)
        def _(group):
            for win_col in range(4):
                attention_group(qkv, mixed, bias.at[which], ones, win_row, win_col, group)

    @pl.loop(0, HP)
    def _(i):
        row = pl.multiple_of((WIN - row_shift + i) * SPAN_C, SPAN_C)
        values = pltpu.roll(mixed[pl.ds(row, SPAN_C), :], SPAN_C - WIN + col_shift, 0)
        row_stage[pl.ds(pl.multiple_of((i % 4) * WP, 8), WP), :] = values[:WP]

        @pl.when(i % 4 == 3)
        def _():
            normed[pl.ds(pl.multiple_of((i // 4) * 96, 96), 96), :] = row_stage[...].astype(BF16)

    copies[2].wait()

    @pl.loop(0, D // COLS)
    def _(n):
        cols = pl.ds(pl.multiple_of(n * COLS, COLS), COLS)

        @pl.loop(0, TOKENS // 256)
        def _(m):
            rows = pl.ds(pl.multiple_of(m * 256, 256), 256)
            mixed[rows, cols] = jnp.dot(
                normed[rows, :], proj_weight[:, cols], preferred_element_type=F32
            )

    @pl.loop(0, HP // 2)
    def _(pair):
        rows = []
        for half in range(2):
            i = pair * 2 + half
            change = mixed[pl.ds(pl.multiple_of(i * WP, 8), WP), :]
            updated = (change + ext[WIN + i, WIN : WIN + WP, :]).astype(BF16).astype(F32)
            rows.append(layer_norm(updated, out_gain_ref[...]))
        both = jnp.concatenate(rows, axis=0).astype(BF16)
        normed[pl.ds(pl.multiple_of(pair * 2 * WP, 2 * WP), 2 * WP), :] = both

    copies[3].wait()

    @pl.loop(0, CELLS // 2)
    def _(n):
        cols = pl.ds(pl.multiple_of(n * COLS, COLS), COLS)

        @pl.loop(0, 3)
        def _(m):
            rows = pl.ds(pl.multiple_of(m * 256, 256), 256)
            cells = jnp.dot(
                normed[rows, :], unembed_weight[:, cols], preferred_element_type=F32
            ).astype(BF16)
            cells = jnp.dot(cells, read_pair[...], preferred_element_type=F32)
            pair = jnp.concatenate(
                [cells[:, :CH].reshape(32, 8, CH), cells[:, CH:].reshape(32, 8, CH)], axis=1
            ).astype(BF16)
            decoded[pl.ds(m * 32, 32), pl.ds(pl.multiple_of(n * 16, 16), 16), :] = pair

    cell_iota = lax.broadcasted_iota(jnp.int32, (TILE, TILE), 0)

    @pl.loop(0, BLOCKS // GROUP)
    def _(part):
        for b in range(GROUP):
            block = part * GROUP + b
            cells = cells_ref[pl.ds(block, 1), :]
            one_hot = jnp.where(cell_iota == cells, 1.0, 0.0).astype(BF16)
            out_stage[block] = lax.dot_general(
                one_hot, decoded[tiles_ref[block]], (((0,), (0,)), ((), ())), preferred_element_type=F32
            ).astype(BF16)
        rows = pl.ds(part * GROUP, GROUP)
        pltpu.make_async_copy(out_stage.at[rows], out_hbm.at[rows], out_sems.at[part]).start()

    @pl.loop(0, BLOCKS // GROUP)
    def _(part):
        rows = pl.ds(part * GROUP, GROUP)
        pltpu.make_async_copy(out_stage.at[rows], out_hbm.at[rows], out_sems.at[part]).wait()


def tail(meta, block_tiles, live_cells, tokens, halos, norm_gain, out_gain, read_weight, qkv_weight, proj_weight, unembed_weight):
    vmem = pl.BlockSpec(memory_space=pltpu.VMEM)
    smem = pl.BlockSpec(memory_space=pltpu.SMEM)
    hbm = pl.BlockSpec(memory_space=pl.ANY)
    return pl.pallas_call(
        tail_kernel,
        in_specs=[smem, smem, vmem, hbm] + [vmem] * 8 + [vmem] * 3 + [hbm] * 3,
        out_specs=hbm,
        out_shape=jax.ShapeDtypeStruct((BLOCKS, TILE, CH), BF16),
        scratch_shapes=[
            pltpu.VMEM((EXT_R, EXT_C, D), F32),
            pltpu.VMEM((REGION, D), F32),
            pltpu.VMEM((REGION, D), BF16),
            pltpu.VMEM((REGION, 3 * D), BF16),
            pltpu.VMEM((96, D), F32),
            pltpu.VMEM((TILES, TILE, CH), BF16),
            pltpu.VMEM((BLOCKS, TILE, CH), BF16),
            pltpu.VMEM((2, WIN_TOK, LANES), F32),
            pltpu.VMEM((4 * WIN_TOK, LANES), BF16),
            pltpu.VMEM((2 * CH, 2 * CH), BF16),
            pltpu.VMEM((D, 3 * D), BF16),
            pltpu.VMEM((D, D), BF16),
            pltpu.VMEM((D, 2 * D), BF16),
            pltpu.SemaphoreType.DMA((4,)),
            pltpu.SemaphoreType.DMA((BLOCKS // GROUP,)),
        ],
        compiler_params=pltpu.CompilerParams(vmem_limit_bytes=VMEM_LIMIT),
        cost_estimate=pl.CostEstimate(flops=16 * 10**9, bytes_accessed=24 * 10**6, transcendentals=3 * 10**6),
        name="attention_decode",
    )(
        meta, block_tiles, live_cells, tokens, *halos,
        norm_gain, out_gain, read_weight, qkv_weight, proj_weight, unembed_weight,
    )


def exchange(west, east, north, south, nw, ne, sw, se):
    lon, lat = lax.axis_size("lon"), lax.axis_size("lat")

    def send(value, lon_step, lat_step):
        pairs = [
            (i * lat + j, (i + lon_step) % lon * lat + (j + lat_step) % lat)
            for i in range(lon)
            for j in range(lat)
        ]
        return lax.ppermute(value, ("lon", "lat"), pairs)

    from_north, from_south = send(south, 0, 1), send(north, 0, -1)
    from_nw, from_ne = send(se, 1, 1), send(sw, -1, 1)
    from_sw, from_se = send(ne, 1, -1), send(nw, -1, -1)
    from_west, from_east = send(east, 1, 0), send(west, -1, 0)
    return from_west, from_east, from_north, from_south, from_nw, from_ne, from_sw, from_se


def per_device(
    obs_values,
    obs_weights,
    block_counts,
    obs_cells,
    block_tiles,
    shift_offsets,
    embed_weight,
    patch_weight,
    norm_gain,
    qkv_weight,
    proj_weight,
    out_gain,
    unembed_weight,
    read_weight,
):
    slot_iota = lax.broadcasted_iota(jnp.int32, obs_weights.shape, 2)
    live = slot_iota < block_counts[:, :, None]
    embedded = jax.nn.gelu(
        jnp.einsum("bsrf,fc->bsrc", obs_values, embed_weight, preferred_element_type=F32)
    )
    outgoing = jnp.where(live[..., None], embedded * obs_weights[..., None], DEAD).astype(BF16)
    received = lax.all_to_all(outgoing, ("lon", "lat"), split_axis=0, concat_axis=0, tiled=True)
    block_tiles = block_tiles.reshape(BLOCKS)
    tokens, *edges, live_cells = grid_tokens(
        block_tiles, obs_cells.reshape(BLOCKS, TILE), received.reshape(BLOCKS, TILE, CH), patch_weight
    )
    halos = exchange(*edges)
    lat_index = lax.axis_index("lat")
    last = lax.axis_size("lat") - 1
    special = jnp.where(lat_index == 0, 0, jnp.where(lat_index == last, 4, -1)).astype(jnp.int32)
    meta = jnp.concatenate([shift_offsets, special.reshape(1)])
    sampled = tail(
        meta, block_tiles, live_cells, tokens.reshape(HP, WP, D), halos,
        norm_gain.reshape(1, D), out_gain.reshape(1, D), read_weight, qkv_weight, proj_weight, unembed_weight,
    )
    returned = lax.all_to_all(
        sampled.reshape(BLOCKS, 1, TILE, CH), ("lon", "lat"), split_axis=0, concat_axis=0, tiled=True
    )
    return returned


def solution(mesh):
    rows = ("lon", "lat")
    in_specs = (
        P(rows, None, None, None),
        P(rows, None, None),
        P(rows, None),
        P(rows, None, None),
        P(rows, None),
    ) + (P(),) * 9
    out_specs = P(rows, None, None, None)
    return jax.shard_map(
        per_device, mesh=mesh, in_specs=in_specs, out_specs=out_specs, check_vma=False
    )
```

```python
import jax
import jax.numpy as jnp
from jax import lax
from jax.experimental import pallas as pl
from jax.experimental.pallas import tpu as pltpu
from jax.sharding import PartitionSpec as P

CH = 128
D = 1024
HEAD = 32
CELLS = 16
WIN = 8
TILE = 128
HP = 32
WP = 24
TILES = 96
TOKENS = HP * WP
BLOCKS = 128
GROUP = 16
SPAN_R = HP + WIN
SPAN_C = WP + WIN
EXT_R = HP + 2 * WIN
WIN_TOK = WIN * WIN
LANES = 128
COLS = 256
DEAD = 1e30
GELU = 0.7978845608028654
DEAD_LIMIT = 1e6
MIB = 1024 * 1024
F32 = jnp.float32
BF16 = jnp.bfloat16


VMEM_SPEC = pl.BlockSpec(memory_space=pltpu.VMEM)
SMEM_SPEC = pl.BlockSpec(memory_space=pltpu.SMEM)
HBM_SPEC = pl.BlockSpec(memory_space=pl.ANY)


def layer_norm(values, gain_vector):
    row_mean = jnp.mean(values, axis=-1, keepdims=True)
    centered = values - row_mean
    variance = jnp.mean(centered * centered, axis=-1, keepdims=True)
    return centered * lax.rsqrt(variance + 1e-05) * gain_vector


def embed_kernel(counts_ref, weights_ref, embed_ref, values_hbm, out_hbm, values, out, in_sems, out_sems):
    parts = BLOCKS // GROUP

    def arrival(part):
        rows = pl.ds(part * GROUP, GROUP)
        return pltpu.make_async_copy(values_hbm.at[rows], values.at[rows], in_sems.at[part])

    def leave(part):
        rows = pl.ds(part * GROUP, GROUP)
        return pltpu.make_async_copy(out.at[rows], out_hbm.at[rows], out_sems.at[part])

    for part in range(parts):
        arrival(part).start()
    slot_iota = lax.broadcasted_iota(jnp.int32, (TILE, CH), 0)

    @pl.loop(0, parts)
    def _(part):
        first = pl.multiple_of(part * GROUP, GROUP)
        columns = (weights_ref[pl.ds(first, GROUP), :] * 0.5).T
        arrival(part).wait()
        for b in range(GROUP):
            raw = jnp.dot(values[first + b], embed_ref[...], preferred_element_type=F32)
            inner = jnp.tanh(raw * (GELU + GELU * 0.044715 * (raw * raw)))
            embedded = raw * columns[:, b : b + 1] * (1.0 + inner)
            out[first + b] = jnp.where(slot_iota < counts_ref[first + b], embedded, DEAD).astype(BF16)
        leave(part).start()

    for part in range(parts):
        leave(part).wait()


def embed(block_counts, obs_values, obs_weights, embed_weight):
    return pl.pallas_call(
        embed_kernel,
        in_specs=[SMEM_SPEC, VMEM_SPEC, VMEM_SPEC, HBM_SPEC],
        out_specs=HBM_SPEC,
        out_shape=jax.ShapeDtypeStruct((BLOCKS, TILE, CH), BF16),
        scratch_shapes=[
            pltpu.VMEM((BLOCKS, TILE, CH), BF16),
            pltpu.VMEM((BLOCKS, TILE, CH), BF16),
            pltpu.SemaphoreType.DMA((BLOCKS // GROUP,)),
            pltpu.SemaphoreType.DMA((BLOCKS // GROUP,)),
        ],
        compiler_params=pltpu.CompilerParams(vmem_limit_bytes=60 * MIB),
        cost_estimate=pl.CostEstimate(flops=6 * 10**8, bytes_accessed=8 * 10**6, transcendentals=2 * 10**6),
        name="embed",
    )(block_counts, obs_weights, embed_weight, obs_values)


def grid_kernel(
    tiles_ref, cells_ref, gain_ref, received_hbm, patch_hbm,
    tokens_ref, normed_ref, west_ref, east_ref, north_ref, south_ref, live_cells_ref,
    received, cell_sums, patch_rows, patch_weight, normed, sems,
):
    parts = BLOCKS // GROUP

    def arrival(part):
        rows = pl.ds(part * GROUP, GROUP)
        return pltpu.make_async_copy(received_hbm.at[rows], received.at[rows], sems.at[part])

    for part in range(parts):
        arrival(part).start()
    weight_copy = pltpu.make_async_copy(patch_hbm, patch_weight, sems.at[parts])
    weight_copy.start()

    @pl.loop(0, TILES, unroll=2)
    def _(tile):
        cell_sums[tile] = jnp.zeros((TILE, CH), F32)

    cell_iota = lax.broadcasted_iota(jnp.int32, (TILE, TILE), 0)
    slot_iota = lax.broadcasted_iota(jnp.int32, (1, TILE), 1).astype(F32)

    @pl.loop(0, parts)
    def _(part):
        arrival(part).wait()
        first = pl.multiple_of(part * GROUP, GROUP)
        all_cells = cells_ref[pl.ds(first, GROUP), :]
        all_cells = (all_cells & 15) * 8 + (all_cells >> 4)
        live_rows = []
        for b in range(GROUP):
            cells = all_cells[b : b + 1, :]
            block = received[first + b]
            live = block < jnp.asarray(DEAD_LIMIT, BF16)
            block = jnp.where(live, block, jnp.zeros_like(block))
            count = jnp.sum(jnp.where(live, 1.0, 0.0).astype(F32), axis=0, keepdims=True)
            live_rows.append(jnp.where(slot_iota < count, cells, -1))
            one_hot = jnp.where(cell_iota == cells, 1.0, 0.0).astype(BF16)
            tile = tiles_ref[first + b]
            cell_sums[tile] += jnp.dot(one_hot, block, preferred_element_type=F32)
        live_cells_ref[pl.ds(first, GROUP), :] = jnp.concatenate(live_rows, axis=0)

    weight_copy.wait()

    @pl.loop(0, 3, unroll=3)
    def _(m):
        rows = pl.ds(pl.multiple_of(m * 256, 256), 256)
        tiles = cell_sums[pl.ds(m * 32, 32)].reshape(32, CELLS, 8, CH)
        for cell in range(CELLS):
            patch_rows[rows, cell * CH : (cell + 1) * CH] = tiles[:, cell].reshape(256, CH).astype(BF16)
        part = jnp.dot(patch_rows[rows, :], patch_weight[...], preferred_element_type=F32).astype(BF16)
        tokens_ref[rows, :] = part
        values = layer_norm(part.astype(F32), gain_ref[...])
        normed[rows, :] = values
        normed_ref[rows, :] = values.astype(BF16)

    def edge(row, col):
        first = normed[pl.ds(pl.multiple_of(row * WP + col, 8), WIN), :]
        second = normed[pl.ds(pl.multiple_of((row + 1) * WP + col, 8), WIN), :]
        return jnp.concatenate([first, second], axis=0).astype(BF16)

    @pl.loop(0, HP // 2, unroll=2)
    def _(pair):
        rows = pl.ds(pl.multiple_of(pair * 16, 16), 16)
        west_ref[rows, :] = edge(pair * 2, 0)
        east_ref[rows, :] = edge(pair * 2, WP - WIN)

    @pl.loop(0, WIN // 2, unroll=2)
    def _(pair):
        for col in range(3):
            rows = pl.ds(pl.multiple_of(col * WIN_TOK + pair * 16, 16), 16)
            north_ref[rows, :] = edge(pair * 2, col * WIN)
            south_ref[rows, :] = edge(HP - WIN + pair * 2, col * WIN)


def grid_tokens(block_tiles, obs_cells, norm_gain, received, patch_weight):
    whole = lambda rows: jax.ShapeDtypeStruct((rows, D), BF16)
    outs = [whole(n) for n in (TOKENS, TOKENS, WIN * HP, WIN * HP, WIN * WP, WIN * WP)]
    outs.append(jax.ShapeDtypeStruct((BLOCKS, TILE), jnp.int32))
    return pl.pallas_call(
        grid_kernel,
        in_specs=[SMEM_SPEC, VMEM_SPEC, VMEM_SPEC, HBM_SPEC, HBM_SPEC],
        out_specs=[VMEM_SPEC] * len(outs),
        scratch_shapes=[
            pltpu.VMEM((BLOCKS, TILE, CH), BF16),
            pltpu.VMEM((TILES, TILE, CH), F32),
            pltpu.VMEM((TOKENS, CELLS * CH), BF16),
            pltpu.VMEM((CELLS * CH, D), BF16),
            pltpu.VMEM((TOKENS, D), F32),
            pltpu.SemaphoreType.DMA((BLOCKS // GROUP + 1,)),
        ],
        out_shape=outs,
        compiler_params=pltpu.CompilerParams(vmem_limit_bytes=40 * MIB),
        cost_estimate=pl.CostEstimate(flops=4 * 10**9, bytes_accessed=14 * 10**6, transcendentals=0),
        name="grid_tokens",
    )(block_tiles, obs_cells, norm_gain, received, pltpu.with_memory_space_constraint(patch_weight, pltpu.HBM))


INNER = (1, 1, 3, (1, 2))
EDGES = (0, 4, 2, (1, 2))
SIDES = (0, 1, 5, (0, 3))


def slots_of(windows):
    return windows[2] * len(windows[3])


def place(source, first, ext, across, rows, row, col, width):
    @pl.loop(0, rows // 2, unroll=2)
    def _(pair):
        both = source[pl.ds(pl.multiple_of(first + pair * 2 * width, 16), 2 * width), :].astype(F32)
        at = (row + pair * 2) * across + col
        ext[pl.ds(pl.multiple_of(at, 8), width), :] = both[:width]
        ext[pl.ds(pl.multiple_of(at + across, 8), width), :] = both[width:]


def attend(windows, meta_ref, ext, qkv_hbm, picked, qkv, qkv_weight, bias, ones, weight_sems, fill, store, later=None):
    row_shift, col_shift, special = meta_ref[0], meta_ref[1], meta_ref[2]
    first, stride, count, cols = windows
    total = slots_of(windows) * WIN_TOK

    def weights(part):
        cols = pl.ds(pl.multiple_of(part * D, D), D)
        return pltpu.make_async_copy(qkv_hbm.at[:, cols], qkv_weight.at[:, cols], weight_sems.at[part])

    for part in range(3):
        weights(part).start()
    ones[...] = (
        lax.broadcasted_iota(jnp.int32, (4 * WIN_TOK, LANES), 0) // WIN_TOK
        == lax.broadcasted_iota(jnp.int32, (4 * WIN_TOK, LANES), 1) // HEAD
    ).astype(F32).astype(BF16)
    row_step = fill()

    @pl.loop(0, count * 4, unroll=2)
    def _(pair):
        step, quarter = pair // 4, pair % 4
        row = row_step * step + quarter * 2 + row_shift
        for index, col in enumerate(cols):
            rows = []
            for half in range(2):
                if windows is SIDES:
                    at = pl.multiple_of((row + half) * 4 * WIN + index * 2 * WIN, 2 * WIN)
                    rows.append(pltpu.roll(ext[pl.ds(at, 2 * WIN), :], 2 * WIN - col_shift, 0)[:WIN])
                else:
                    at = pl.multiple_of((row + half) * WP, 8)
                    around = pltpu.roll(ext[pl.ds(at, WP), :], WP - col_shift, 0)
                    rows.append(around[index * WIN : (index + 1) * WIN])
            at = (step * len(cols) + index) * WIN_TOK + quarter * 16
            picked[pl.ds(pl.multiple_of(at, 16), 16), :] = jnp.concatenate(rows, axis=0).astype(BF16)

    block = total // 2 if total > 512 else total

    @pl.loop(0, 3)
    def _(n):
        weights(n).wait()
        lanes = pl.ds(pl.multiple_of(n * D, D), D)

        @pl.loop(0, total // block, unroll=total // block)
        def _(m):
            rows = pl.ds(pl.multiple_of(m * block, block), block)
            qkv[rows, lanes] = jnp.dot(
                picked[rows, :], qkv_weight[:, lanes], preferred_element_type=F32
            ).astype(BF16)

    if later is not None:
        later()
    edge_rows = first == 0
    if edge_rows:

        @pl.loop(0, WIN)
        def _(i):
            query_flag = jnp.where(i >= WIN - row_shift, 1, 0)
            key_row = (lax.broadcasted_iota(jnp.int32, (WIN, LANES), 1) % WIN_TOK) // WIN
            key_flag = jnp.where(key_row >= WIN - row_shift, 1, 0)
            bias[1, pl.ds(pl.multiple_of(i * WIN, 8), WIN), :] = jnp.where(key_flag == query_flag, 0.0, 1.0)

        bias[0] = jnp.zeros((WIN_TOK, LANES), F32)

    @pl.loop(0, count, unroll=count)
    def _(step):
        mask = bias.at[jnp.where(first + stride * step == special, 1, 0)] if edge_rows else None

        @pl.loop(0, D // LANES, unroll=8)
        def _(group):
            for index in range(len(cols)):
                result = attention_group(qkv, mask, ones, step * len(cols) + index, group)
                lanes = pl.ds(pl.multiple_of(group * LANES, LANES), LANES)
                for i in range(WIN):
                    store(step, index, i, lanes, result[i * WIN : (i + 1) * WIN])


def attention_group(qkv, mask, ones, slot, group):
    rows = pl.ds(pl.multiple_of(slot * WIN_TOK, WIN_TOK), WIN_TOK)
    lanes = lambda part: pl.ds(pl.multiple_of(part * D + group * LANES, LANES), LANES)
    query, key, value = (qkv[rows, lanes(part)] for part in range(3))
    head_of_lane = lax.broadcasted_iota(jnp.int32, (WIN_TOK, LANES), 1) // HEAD
    zero = jnp.zeros((WIN_TOK, LANES), BF16)
    spread = lambda x: jnp.concatenate([jnp.where(head_of_lane == h, x, zero) for h in range(4)], axis=0)
    scores = lax.dot_general(
        query, spread(key), (((1,), (1,)), ((), ())), preferred_element_type=F32
    ) * HEAD ** (-0.5)
    low = lax.broadcasted_iota(jnp.int32, (WIN_TOK, LANES), 1) < WIN_TOK
    parts = []
    for half in range(2):
        part = scores[:, half * LANES : (half + 1) * LANES]
        if mask is not None:
            part = jnp.where(mask[...] < 0.5, part, -1000000000.0)
        low_max = jnp.max(jnp.where(low, part, -jnp.inf), axis=-1, keepdims=True)
        high_max = jnp.max(jnp.where(low, -jnp.inf, part), axis=-1, keepdims=True)
        parts.append(jnp.exp(part - jnp.where(low, low_max, high_max)).astype(BF16))
    weights = jnp.concatenate(parts, axis=1)
    both = jnp.dot(weights, jnp.concatenate([spread(value), ones[...]], axis=1), preferred_element_type=F32)
    return (both[:, :LANES] / both[:, LANES:]).astype(BF16).astype(F32)


def windows_kernel(windows, *refs):
    meta_ref, *sources, qkv_hbm, out, ext, picked, qkv, qkv_weight, bias, ones, weight_sems = refs

    def fill():
        if windows is INNER:
            place(sources[0], 0, ext, WP, HP, 0, 0, WP)
            return WIN
        for index, source in enumerate(sources):
            for col in range(3):
                place(source, col * WIN_TOK, ext, WP, WIN, index * WIN, col * WIN, WIN)
        return 2 * WIN

    def store(step, index, i, lanes, value):
        out[step * WIN + i, index * WIN : (index + 1) * WIN, lanes] = value

    attend(windows, meta_ref, ext, qkv_hbm, picked, qkv, qkv_weight, bias, ones, weight_sems, fill, store)


def attend_scratch(windows):
    rows = slots_of(windows) * WIN_TOK
    return [
        pltpu.VMEM((EXT_R * 4 * WIN if windows is SIDES else HP * WP, D), F32),
        pltpu.VMEM((rows, D), BF16),
        pltpu.VMEM((rows, 3 * D), BF16),
        pltpu.VMEM((D, 3 * D), BF16),
        pltpu.VMEM((2, WIN_TOK, LANES), F32),
        pltpu.VMEM((4 * WIN_TOK, LANES), BF16),
        pltpu.SemaphoreType.DMA((3,)),
    ]


def attend_windows(windows, name, meta, sources, qkv_weight):
    rows = slots_of(windows) * WIN_TOK
    return pl.pallas_call(
        lambda *refs: windows_kernel(windows, *refs),
        in_specs=[SMEM_SPEC] + [VMEM_SPEC] * len(sources) + [HBM_SPEC],
        out_specs=VMEM_SPEC,
        out_shape=jax.ShapeDtypeStruct((windows[2] * WIN, 2 * WIN, D), F32),
        scratch_shapes=attend_scratch(windows),
        compiler_params=pltpu.CompilerParams(vmem_limit_bytes=28 * MIB),
        cost_estimate=pl.CostEstimate(
            flops=rows * D * 3 * D * 3, bytes_accessed=12 * 10**6, transcendentals=rows * 2048
        ),
        name=name,
    )(meta, *sources, qkv_weight)


def tail_kernel(
    meta_ref, tiles_ref, cells_ref, tokens_hbm, west_ref, east_ref, from_west_ref, from_east_ref,
    inner_hbm, edges_hbm, out_gain_ref, read_ref, qkv_hbm, proj_hbm, unembed_hbm,
    out_hbm,
    ext, picked, qkv, qkv_weight, bias, ones, weight_sems,
    mixed, mixed_rows, tokens, decoded, out_stage, read_pair,
    proj_weight, unembed_weight, in_sems, out_sems,
):
    row_shift, col_shift = meta_ref[0], meta_ref[1]
    inner_cols = pl.ds(WIN, 2 * WIN)
    moves = (
        (inner_hbm, mixed.at[pl.ds(WIN, 3 * WIN), inner_cols, :]),
        (edges_hbm.at[pl.ds(0, WIN)], mixed.at[pl.ds(0, WIN), inner_cols, :]),
        (edges_hbm.at[pl.ds(WIN, WIN)], mixed.at[pl.ds(SPAN_R - WIN, WIN), inner_cols, :]),
        (proj_hbm, proj_weight),
        (tokens_hbm, tokens),
        (unembed_hbm, unembed_weight),
    )
    copies = [pltpu.make_async_copy(src, dst, in_sems.at[i]) for i, (src, dst) in enumerate(moves)]

    def fill():
        place(from_west_ref, 0, ext, 4 * WIN, EXT_R, 0, 0, WIN)
        place(west_ref, 0, ext, 4 * WIN, EXT_R, 0, WIN, WIN)
        place(east_ref, 0, ext, 4 * WIN, EXT_R, 0, 2 * WIN, WIN)
        place(from_east_ref, 0, ext, 4 * WIN, EXT_R, 0, 3 * WIN, WIN)
        read_pair[...] = jnp.zeros((2 * CH, 2 * CH), BF16)
        read_pair[:CH, :CH] = read_ref[...]
        read_pair[CH:, CH:] = read_ref[...]
        return WIN

    def store(step, index, i, lanes, value):
        mixed[step * WIN + i, index * 3 * WIN : index * 3 * WIN + WIN, lanes] = value

    def later():
        for copy in copies:
            copy.start()

    attend(SIDES, meta_ref, ext, qkv_hbm, picked, qkv, qkv_weight, bias, ones, weight_sems, fill, store, later)
    for copy in copies[:5]:
        copy.wait()

    @pl.loop(0, HP // 2, unroll=2)
    def _(pair):
        rows = [
            pltpu.roll(mixed[WIN - row_shift + pair * 2 + half], SPAN_C - WIN + col_shift, 0)[:WP]
            for half in range(2)
        ]
        mixed_rows[pl.ds(pl.multiple_of(pair * 2 * WP, 2 * WP), 2 * WP), :] = jnp.concatenate(
            rows, axis=0
        ).astype(BF16)

    @pl.loop(0, TOKENS // 256, unroll=3)
    def _(m):
        rows = pl.ds(pl.multiple_of(m * 256, 256), 256)
        change = jnp.dot(mixed_rows[rows, :], proj_weight[...], preferred_element_type=F32)
        updated = (change + tokens[rows, :].astype(F32)).astype(BF16).astype(F32)
        mixed_rows[rows, :] = layer_norm(updated, out_gain_ref[...]).astype(BF16)

    copies[5].wait()

    @pl.loop(0, 2)
    def _(n):
        cols = pl.ds(pl.multiple_of(n * D, D), D)

        @pl.loop(0, 3, unroll=3)
        def _(m):
            rows = pl.ds(pl.multiple_of(m * 256, 256), 256)
            quad = jnp.dot(
                mixed_rows[rows, :], unembed_weight[:, cols], preferred_element_type=F32
            ).astype(BF16)
            for k in range(4):
                cells = jnp.dot(
                    quad[:, k * COLS : (k + 1) * COLS], read_pair[...], preferred_element_type=F32
                )
                pair = jnp.concatenate(
                    [cells[:, :CH].reshape(32, 8, CH), cells[:, CH:].reshape(32, 8, CH)], axis=1
                ).astype(BF16)
                place_at = pl.multiple_of(n * 64 + k * 16, 16)
                decoded[pl.ds(m * 32, 32), pl.ds(place_at, 16), :] = pair

    cell_iota = lax.broadcasted_iota(jnp.int32, (TILE, TILE), 0)

    def leave(part):
        return pltpu.make_async_copy(
            out_stage.at[part % 2], out_hbm.at[pl.ds(part * GROUP, GROUP)], out_sems.at[part % 2]
        )

    @pl.loop(0, BLOCKS // GROUP)
    def _(part):
        @pl.when(part >= 2)
        def _():
            leave(part - 2).wait()

        for b in range(GROUP):
            block = part * GROUP + b
            cells = cells_ref[pl.ds(block, 1), :]
            one_hot = jnp.where(cell_iota == cells, 1.0, 0.0).astype(BF16)
            out_stage[part % 2, b] = lax.dot_general(
                one_hot, decoded[tiles_ref[block]], (((0,), (0,)), ((), ())), preferred_element_type=F32
            ).astype(BF16)
        leave(part).start()

    for part in range(BLOCKS // GROUP - 2, BLOCKS // GROUP):
        leave(part).wait()


def tail(meta, block_tiles, live_cells, tokens, sides, mixed_parts, out_gain, read_weight, qkv_weight, proj_weight, unembed_weight):
    return pl.pallas_call(
        tail_kernel,
        in_specs=[SMEM_SPEC, SMEM_SPEC] + [VMEM_SPEC, HBM_SPEC] + [VMEM_SPEC] * 4 + [HBM_SPEC] * 2 + [VMEM_SPEC] * 2 + [HBM_SPEC] * 3,
        out_specs=HBM_SPEC,
        out_shape=jax.ShapeDtypeStruct((BLOCKS, TILE, CH), BF16),
        scratch_shapes=attend_scratch(SIDES)
        + [
            pltpu.VMEM((SPAN_R, SPAN_C, D), F32),
            pltpu.VMEM((TOKENS, D), BF16),
            pltpu.VMEM((TOKENS, D), BF16),
            pltpu.VMEM((TILES, TILE, CH), BF16),
            pltpu.VMEM((2, GROUP, TILE, CH), BF16),
            pltpu.VMEM((2 * CH, 2 * CH), BF16),
            pltpu.VMEM((D, D), BF16),
            pltpu.VMEM((D, 2 * D), BF16),
            pltpu.SemaphoreType.DMA((6,)),
            pltpu.SemaphoreType.DMA((2,)),
        ],
        compiler_params=pltpu.CompilerParams(vmem_limit_bytes=46 * MIB),
        cost_estimate=pl.CostEstimate(flops=12 * 10**9, bytes_accessed=28 * 10**6, transcendentals=10**6),
        name="sides_decode",
    )(
        meta, block_tiles, live_cells, pltpu.with_memory_space_constraint(tokens, pltpu.HBM), *sides, *mixed_parts,
        out_gain, read_weight, qkv_weight, proj_weight, unembed_weight,
    )


def send(value, lon_step, lat_step):
    lon, lat = lax.axis_size("lon"), lax.axis_size("lat")
    pairs = [
        (i * lat + j, (i + lon_step) % lon * lat + (j + lat_step) % lat) for i in range(lon) for j in range(lat)
    ]
    return lax.ppermute(value, ("lon", "lat"), pairs)


def attention_and_decode(meta, block_tiles, live_cells, tokens, normed, west, east, north, south, out_gain, read_weight, qkv_weight, proj_weight, unembed_weight):
    from_north, from_south = send(south, 0, 1), send(north, 0, -1)
    inner = attend_windows(INNER, "inner_windows", meta, (normed,), qkv_weight)
    from_north, from_south, inner = lax.optimization_barrier((from_north, from_south, inner))
    west = jnp.concatenate([from_north[:WIN_TOK], west, from_south[:WIN_TOK]], axis=0)
    east = jnp.concatenate([from_north[2 * WIN_TOK :], east, from_south[2 * WIN_TOK :]], axis=0)
    from_west, from_east = send(east, 1, 0), send(west, -1, 0)
    edges = attend_windows(EDGES, "edge_windows", meta, (from_north, north, south, from_south), qkv_weight)
    from_west, from_east, edges = lax.optimization_barrier((from_west, from_east, edges))
    return tail(
        meta, block_tiles, live_cells, tokens, (west, east, from_west, from_east), (inner, edges),
        out_gain, read_weight, qkv_weight, proj_weight, unembed_weight,
    )


def per_device(
    obs_values,
    obs_weights,
    block_counts,
    obs_cells,
    block_tiles,
    shift_offsets,
    embed_weight,
    patch_weight,
    norm_gain,
    qkv_weight,
    proj_weight,
    out_gain,
    unembed_weight,
    read_weight,
):
    outgoing = embed(
        block_counts.reshape(BLOCKS), obs_values.reshape(BLOCKS, TILE, CH), obs_weights.reshape(BLOCKS, TILE), embed_weight
    ).reshape(BLOCKS, 1, TILE, CH)
    received = lax.all_to_all(outgoing, ("lon", "lat"), split_axis=0, concat_axis=0, tiled=True)
    block_tiles = block_tiles.reshape(BLOCKS)
    tokens, normed, west, east, north, south, live_cells = grid_tokens(
        block_tiles, obs_cells.reshape(BLOCKS, TILE), norm_gain.reshape(1, D),
        received.reshape(BLOCKS, TILE, CH), patch_weight,
    )
    lat_index = lax.axis_index("lat")
    last = lax.axis_size("lat") - 1
    special = jnp.where(lat_index == 0, 0, jnp.where(lat_index == last, 4, -1)).astype(jnp.int32)
    meta = jnp.concatenate([shift_offsets, special.reshape(1)])
    sampled = attention_and_decode(
        meta, block_tiles, live_cells, tokens, normed, west, east, north, south,
        out_gain.reshape(1, D), read_weight, qkv_weight, proj_weight, unembed_weight,
    )
    returned = lax.all_to_all(
        sampled.reshape(BLOCKS, 1, TILE, CH), ("lon", "lat"), split_axis=0, concat_axis=0, tiled=True
    )
    return returned


def solution(mesh):
    rows = ("lon", "lat")
    in_specs = (
        P(rows, None, None, None),
        P(rows, None, None),
        P(rows, None),
        P(rows, None, None),
        P(rows, None),
    ) + (P(),) * 9
    out_specs = P(rows, None, None, None)
    return jax.shard_map(
        per_device, mesh=mesh, in_specs=in_specs, out_specs=out_specs, check_vma=False
    )
```

```python
import jax
import jax.numpy as jnp
from jax import lax
from jax.experimental import pallas as pl
from jax.experimental.pallas import tpu as pltpu
from jax.sharding import PartitionSpec as P

CH = 128
D = 1024
HEAD = 32
CELLS = 16
WIN = 8
TILE = 128
HP = 32
WP = 24
TILES = 96
TOKENS = HP * WP
BLOCKS = 128
GROUP = 16
SPAN_R = HP + WIN
SPAN_C = WP + WIN
EXT_R = HP + 2 * WIN
WIN_TOK = WIN * WIN
LANES = 128
COLS = 256
DEAD = 1e30
GELU = 0.7978845608028654
EXCLUDED = -1e9 * HEAD**0.5
EXP_SCALE = 1.4426950408889634 * HEAD**-0.5
DEAD_LIMIT = 1e6
MIB = 1024 * 1024
F32 = jnp.float32
BF16 = jnp.bfloat16


VMEM_SPEC = pl.BlockSpec(memory_space=pltpu.VMEM)
SMEM_SPEC = pl.BlockSpec(memory_space=pltpu.SMEM)
HBM_SPEC = pl.BlockSpec(memory_space=pl.ANY)


def in_hbm(value):
    return pltpu.with_memory_space_constraint(value, pltpu.HBM)


def layer_norm(values, gain_vector):
    row_mean = jnp.mean(values, axis=-1, keepdims=True)
    centered = values - row_mean
    variance = jnp.mean(centered * centered, axis=-1, keepdims=True)
    return centered * lax.rsqrt(variance + 1e-05) * gain_vector


def embed_kernel(counts_ref, weights_ref, embed_ref, values_hbm, out, values, in_sems):
    parts = BLOCKS // GROUP

    def arrival(part):
        rows = pl.ds(part * GROUP, GROUP)
        return pltpu.make_async_copy(values_hbm.at[rows], values.at[rows], in_sems.at[part])

    for part in range(parts):
        arrival(part).start()
    slot_iota = lax.broadcasted_iota(jnp.int32, (TILE, CH), 0)

    @pl.loop(0, parts)
    def _(part):
        first = pl.multiple_of(part * GROUP, GROUP)
        columns = (weights_ref[pl.ds(first, GROUP), :] * 0.5).T
        arrival(part).wait()
        for b in range(GROUP):
            raw = jnp.dot(values[first + b], embed_ref[...], preferred_element_type=F32)
            inner = jnp.tanh(raw * (GELU + GELU * 0.044715 * (raw * raw)))
            embedded = raw * columns[:, b : b + 1] * (1.0 + inner)
            out[first + b] = jnp.where(slot_iota < counts_ref[first + b], embedded, DEAD).astype(BF16)


def embed(block_counts, obs_values, obs_weights, embed_weight):
    return pl.pallas_call(
        embed_kernel,
        in_specs=[SMEM_SPEC, VMEM_SPEC, VMEM_SPEC, HBM_SPEC],
        out_specs=VMEM_SPEC,
        out_shape=pltpu.VMEM((BLOCKS, TILE, CH), BF16),
        scratch_shapes=[
            pltpu.VMEM((BLOCKS, TILE, CH), BF16),
            pltpu.SemaphoreType.DMA((BLOCKS // GROUP,)),
        ],
        compiler_params=pltpu.CompilerParams(vmem_limit_bytes=24 * MIB),
        cost_estimate=pl.CostEstimate(flops=6 * 10**8, bytes_accessed=8 * 10**6, transcendentals=2 * 10**6),
        name="embed",
    )(in_hbm(block_counts), in_hbm(obs_weights), in_hbm(embed_weight), in_hbm(obs_values))


def grid_kernel(
    tiles_ref, cells_ref, gain_ref, received_hbm, patch_hbm,
    tokens_hbm, normed_hbm, west_ref, east_ref, north_ref, south_ref, live_cells_ref,
    received, cell_sums, patch_rows, patch_weight, tokens, normed, sems, out_sems,
):
    parts = BLOCKS // GROUP

    def arrival(part):
        rows = pl.ds(part * GROUP, GROUP)
        return pltpu.make_async_copy(received_hbm.at[rows], received.at[rows], sems.at[part])

    for part in range(parts):
        arrival(part).start()
    weight_copy = pltpu.make_async_copy(patch_hbm, patch_weight, sems.at[parts])
    weight_copy.start()

    @pl.loop(0, TILES, unroll=2)
    def _(tile):
        cell_sums[tile] = jnp.zeros((TILE, CH), F32)

    cell_iota = lax.broadcasted_iota(jnp.int32, (TILE, TILE), 0)
    slot_iota = lax.broadcasted_iota(jnp.int32, (1, TILE), 1).astype(F32)

    @pl.loop(0, parts)
    def _(part):
        arrival(part).wait()
        first = pl.multiple_of(part * GROUP, GROUP)
        all_cells = cells_ref[pl.ds(first, GROUP), :]
        all_cells = (all_cells & 15) * 8 + (all_cells >> 4)
        live_rows = []
        for b in range(GROUP):
            cells = all_cells[b : b + 1, :]
            block = received[first + b]
            live = block < jnp.asarray(DEAD_LIMIT, BF16)
            block = jnp.where(live, block, jnp.zeros_like(block))
            count = jnp.sum(jnp.where(live, 1.0, 0.0).astype(F32), axis=0, keepdims=True)
            live_rows.append(jnp.where(slot_iota < count, cells, -1))
            one_hot = jnp.where(cell_iota == cells, 1.0, 0.0).astype(BF16)
            tile = tiles_ref[first + b]
            cell_sums[tile] += jnp.dot(one_hot, block, preferred_element_type=F32)
        live_cells_ref[pl.ds(first, GROUP), :] = jnp.concatenate(live_rows, axis=0)

    weight_copy.wait()
    half_rows = HP // 2
    block = half_rows * WP

    def leave(m):
        rows = pl.ds(m * block, block)
        return (
            pltpu.make_async_copy(tokens.at[rows], tokens_hbm.at[rows], out_sems.at[2 * m]),
            pltpu.make_async_copy(normed.at[rows], normed_hbm.at[rows], out_sems.at[2 * m + 1]),
        )

    for m in range(2):
        rows = slice(m * block, (m + 1) * block)
        tiles = cell_sums[m * (TILES // 2) : (m + 1) * (TILES // 2)].reshape(TILES // 2, CELLS, 8, CH)
        for cell in range(CELLS):
            patch_rows[rows, cell * CH : (cell + 1) * CH] = tiles[:, cell].reshape(block, CH).astype(BF16)
        part = jnp.dot(patch_rows[rows, :], patch_weight[...], preferred_element_type=F32).astype(BF16)
        tokens[rows, :] = part
        values = layer_norm(part.astype(F32), gain_ref[...])
        normed[rows, :] = values.astype(BF16)
        values = values.reshape(half_rows, 3, WIN, D)
        side = slice(m * half_rows * WIN, (m + 1) * half_rows * WIN)
        west_ref[side, :] = values[:, 0].reshape(half_rows * WIN, D).astype(BF16)
        east_ref[side, :] = values[:, 2].reshape(half_rows * WIN, D).astype(BF16)
        ends, target = (values[:WIN], north_ref) if m == 0 else (values[half_rows - WIN :], south_ref)
        for col in range(3):
            target[col * WIN_TOK : (col + 1) * WIN_TOK, :] = ends[:, col].reshape(WIN_TOK, D).astype(BF16)
        for copy in leave(m):
            copy.start()

    for m in range(2):
        for copy in leave(m):
            copy.wait()


def grid_tokens(block_tiles, obs_cells, norm_gain, received, patch_weight):
    whole = lambda rows: jax.ShapeDtypeStruct((rows, D), BF16)
    outs = [pltpu.HBM((TOKENS, D), BF16)] * 2 + [whole(n) for n in (WIN * HP, WIN * HP, WIN * WP, WIN * WP)]
    outs.append(jax.ShapeDtypeStruct((BLOCKS, TILE), jnp.int32))
    return pl.pallas_call(
        grid_kernel,
        in_specs=[SMEM_SPEC, VMEM_SPEC, VMEM_SPEC, HBM_SPEC, HBM_SPEC],
        out_specs=[HBM_SPEC] * 2 + [VMEM_SPEC] * (len(outs) - 2),
        scratch_shapes=[
            pltpu.VMEM((BLOCKS, TILE, CH), BF16),
            pltpu.VMEM((TILES, TILE, CH), F32),
            pltpu.VMEM((TOKENS, CELLS * CH), BF16),
            pltpu.VMEM((CELLS * CH, D), BF16),
            pltpu.VMEM((TOKENS, D), BF16),
            pltpu.VMEM((TOKENS, D), BF16),
            pltpu.SemaphoreType.DMA((BLOCKS // GROUP + 1,)),
            pltpu.SemaphoreType.DMA((4,)),
        ],
        out_shape=outs,
        compiler_params=pltpu.CompilerParams(vmem_limit_bytes=40 * MIB),
        cost_estimate=pl.CostEstimate(flops=4 * 10**9, bytes_accessed=14 * 10**6, transcendentals=0),
        name="grid_tokens",
    )(block_tiles, obs_cells, norm_gain, received, in_hbm(patch_weight))


INNER = (1, 1, 3, (1, 2))
EDGES = (0, 4, 2, (1, 2))
SIDES = (0, 1, 5, (0, 3))


def slots_of(windows):
    return windows[2] * len(windows[3])


def place(source, first, ext, across, rows, row, col, width):
    @pl.loop(0, rows // 2, unroll=2)
    def _(pair):
        both = source[pl.ds(pl.multiple_of(first + pair * 2 * width, 16), 2 * width), :].astype(F32)
        at = (row + pair * 2) * across + col
        ext[pl.ds(pl.multiple_of(at, 8), width), :] = both[:width]
        ext[pl.ds(pl.multiple_of(at + across, 8), width), :] = both[width:]


def attend(windows, meta_ref, ext, qkv_hbm, picked, qkv, qkv_weight, bias, ones, weight_sems, fill, store, later=None):
    row_shift, col_shift, special = meta_ref[0], meta_ref[1], meta_ref[2]
    first, stride, count, cols = windows
    total = slots_of(windows) * WIN_TOK

    def weights(part):
        cols = pl.ds(pl.multiple_of(part * D, D), D)
        return pltpu.make_async_copy(qkv_hbm.at[:, cols], qkv_weight.at[:, cols], weight_sems.at[part])

    for part in range(3):
        weights(part).start()
    ones[...] = (
        lax.broadcasted_iota(jnp.int32, (4 * WIN_TOK, LANES), 0) // WIN_TOK
        == lax.broadcasted_iota(jnp.int32, (4 * WIN_TOK, LANES), 1) // HEAD
    ).astype(F32).astype(BF16)
    row_step = fill()

    @pl.loop(0, count * 4, unroll=2)
    def _(pair):
        step, quarter = pair // 4, pair % 4
        row = row_step * step + quarter * 2 + row_shift
        for index, col in enumerate(cols):
            rows = []
            for half in range(2):
                if windows is SIDES:
                    at = pl.multiple_of((row + half) * 4 * WIN + index * 2 * WIN, 2 * WIN)
                    rows.append(pltpu.roll(ext[pl.ds(at, 2 * WIN), :], 2 * WIN - col_shift, 0)[:WIN])
                else:
                    at = pl.multiple_of((row + half) * WP, 8)
                    around = pltpu.roll(ext[pl.ds(at, WP), :], WP - col_shift, 0)
                    rows.append(around[index * WIN : (index + 1) * WIN])
            at = (step * len(cols) + index) * WIN_TOK + quarter * 16
            picked[pl.ds(pl.multiple_of(at, 16), 16), :] = jnp.concatenate(rows, axis=0).astype(BF16)

    block = total // 2 if total > 512 else total

    @pl.loop(0, 3)
    def _(n):
        weights(n).wait()
        lanes = pl.ds(pl.multiple_of(n * D, D), D)

        @pl.loop(0, total // block, unroll=total // block)
        def _(m):
            rows = pl.ds(pl.multiple_of(m * block, block), block)
            qkv[rows, lanes] = jnp.dot(
                picked[rows, :], qkv_weight[:, lanes], preferred_element_type=F32
            ).astype(BF16)

    if later is not None:
        later()
    edge_rows = first == 0
    if edge_rows:

        @pl.loop(0, WIN)
        def _(i):
            query_flag = jnp.where(i >= WIN - row_shift, 1, 0)
            key_row = (lax.broadcasted_iota(jnp.int32, (WIN, LANES), 1) % WIN_TOK) // WIN
            key_flag = jnp.where(key_row >= WIN - row_shift, 1, 0)
            bias[1, pl.ds(pl.multiple_of(i * WIN, 8), WIN), :] = jnp.where(key_flag == query_flag, 0.0, 1.0)

        bias[0] = jnp.zeros((WIN_TOK, LANES), F32)

    for step in range(count):
        row = first + stride * step
        mask = bias.at[jnp.where(row == special, 1, 0)] if row in (0, 4) else None

        @pl.loop(0, D // LANES, unroll=8)
        def _(group, step=step, mask=mask):
            for index in range(len(cols)):
                result = attention_group(qkv, mask, ones, step * len(cols) + index, group)
                lanes = pl.ds(pl.multiple_of(group * LANES, LANES), LANES)
                for i in range(WIN):
                    store(step, index, i, lanes, result[i * WIN : (i + 1) * WIN])


def attention_group(qkv, mask, ones, slot, group):
    rows = pl.ds(pl.multiple_of(slot * WIN_TOK, WIN_TOK), WIN_TOK)
    lanes = lambda part: pl.ds(pl.multiple_of(part * D + group * LANES, LANES), LANES)
    query, key, value = (qkv[rows, lanes(part)] for part in range(3))
    head_of_lane = lax.broadcasted_iota(jnp.int32, (WIN_TOK, LANES), 1) // HEAD
    zero = jnp.zeros((WIN_TOK, LANES), BF16)
    spread = lambda x: jnp.concatenate([jnp.where(head_of_lane == h, x, zero) for h in range(4)], axis=0)
    scores = lax.dot_general(query, spread(key), (((1,), (1,)), ((), ())), preferred_element_type=F32)
    low = lax.broadcasted_iota(jnp.int32, (WIN_TOK, LANES), 1) < WIN_TOK
    parts = []
    for half in range(2):
        part = scores[:, half * LANES : (half + 1) * LANES]
        if mask is not None:
            part = jnp.where(mask[...] < 0.5, part, EXCLUDED)
        low_max = jnp.max(jnp.where(low, part, -jnp.inf), axis=-1, keepdims=True)
        high_max = jnp.max(jnp.where(low, -jnp.inf, part), axis=-1, keepdims=True)
        parts.append(jnp.exp2((part - jnp.where(low, low_max, high_max)) * EXP_SCALE).astype(BF16))
    weights = jnp.concatenate(parts, axis=1)
    both = jnp.dot(weights, jnp.concatenate([spread(value), ones[...]], axis=1), preferred_element_type=F32)
    total = both[:, LANES:]
    inverse = pl.reciprocal(total, approx=True)
    inverse = inverse * (2.0 - total * inverse)
    return (both[:, :LANES] * inverse).astype(BF16).astype(F32)


def windows_kernel(windows, *refs):
    meta_ref, *sources, qkv_hbm, out, ext, picked, qkv, qkv_weight, bias, ones, weight_sems = refs

    def fill():
        if windows is INNER:
            place(sources[0], 0, ext, WP, HP, 0, 0, WP)
            return WIN
        for index, source in enumerate(sources):
            for col in range(3):
                place(source, col * WIN_TOK, ext, WP, WIN, index * WIN, col * WIN, WIN)
        return 2 * WIN

    def store(step, index, i, lanes, value):
        out[step * WIN + i, index * WIN : (index + 1) * WIN, lanes] = value

    attend(windows, meta_ref, ext, qkv_hbm, picked, qkv, qkv_weight, bias, ones, weight_sems, fill, store)


def attend_scratch(windows):
    rows = slots_of(windows) * WIN_TOK
    return [
        pltpu.VMEM((EXT_R * 4 * WIN if windows is SIDES else HP * WP, D), F32),
        pltpu.VMEM((rows, D), BF16),
        pltpu.VMEM((rows, 3 * D), BF16),
        pltpu.VMEM((D, 3 * D), BF16),
        pltpu.VMEM((2, WIN_TOK, LANES), F32),
        pltpu.VMEM((4 * WIN_TOK, LANES), BF16),
        pltpu.SemaphoreType.DMA((3,)),
    ]


def attend_windows(windows, name, meta, sources, qkv_weight):
    rows = slots_of(windows) * WIN_TOK
    return pl.pallas_call(
        lambda *refs: windows_kernel(windows, *refs),
        in_specs=[SMEM_SPEC] + [VMEM_SPEC] * len(sources) + [HBM_SPEC],
        out_specs=VMEM_SPEC,
        out_shape=jax.ShapeDtypeStruct((windows[2] * WIN, 2 * WIN, D), F32),
        scratch_shapes=attend_scratch(windows),
        compiler_params=pltpu.CompilerParams(vmem_limit_bytes=28 * MIB),
        cost_estimate=pl.CostEstimate(
            flops=rows * D * 3 * D * 3, bytes_accessed=12 * 10**6, transcendentals=rows * 2048
        ),
        name=name,
    )(meta, *sources, in_hbm(qkv_weight))


def tail_kernel(
    meta_ref, tiles_ref, cells_ref, tokens_hbm,
    west_ref, east_ref, from_west_ref, from_east_ref, own_west_ref, own_east_ref, west_corners_ref, east_corners_ref,
    inner_hbm, edges_hbm, out_gain_ref, read_ref, qkv_hbm, proj_hbm, unembed_hbm,
    out_ref,
    ext, picked, qkv, qkv_weight, bias, ones, weight_sems,
    mixed, mixed_rows, tokens, decoded, read_pair,
    proj_weight, unembed_weight, in_sems,
):
    row_shift, col_shift = meta_ref[0], meta_ref[1]
    inner_cols = pl.ds(WIN, 2 * WIN)
    moves = (
        (inner_hbm, mixed.at[pl.ds(WIN, 3 * WIN), inner_cols, :]),
        (edges_hbm.at[pl.ds(0, WIN)], mixed.at[pl.ds(0, WIN), inner_cols, :]),
        (edges_hbm.at[pl.ds(WIN, WIN)], mixed.at[pl.ds(SPAN_R - WIN, WIN), inner_cols, :]),
        (proj_hbm, proj_weight),
        (tokens_hbm, tokens),
        (unembed_hbm, unembed_weight),
    )
    copies = [pltpu.make_async_copy(src, dst, in_sems.at[i]) for i, (src, dst) in enumerate(moves)]

    def fill():
        columns = (
            (from_west_ref, west_corners_ref), (west_ref, own_west_ref),
            (east_ref, own_east_ref), (from_east_ref, east_corners_ref),
        )
        for index, (middle, ends) in enumerate(columns):
            place(middle, 0, ext, 4 * WIN, HP, WIN, index * WIN, WIN)
            place(ends, 0, ext, 4 * WIN, WIN, 0, index * WIN, WIN)
            place(ends, WIN_TOK, ext, 4 * WIN, WIN, WIN + HP, index * WIN, WIN)
        read_pair[...] = jnp.zeros((2 * CH, 2 * CH), BF16)
        read_pair[:CH, :CH] = read_ref[...]
        read_pair[CH:, CH:] = read_ref[...]
        return WIN

    def store(step, index, i, lanes, value):
        mixed[step * WIN + i, index * 3 * WIN : index * 3 * WIN + WIN, lanes] = value

    def later():
        for copy in copies:
            copy.start()

    attend(SIDES, meta_ref, ext, qkv_hbm, picked, qkv, qkv_weight, bias, ones, weight_sems, fill, store, later)
    for copy in copies[:5]:
        copy.wait()

    @pl.loop(0, HP // 2, unroll=2)
    def _(pair):
        rows = [
            pltpu.roll(mixed[WIN - row_shift + pair * 2 + half], SPAN_C - WIN + col_shift, 0)[:WP]
            for half in range(2)
        ]
        mixed_rows[pl.ds(pl.multiple_of(pair * 2 * WP, 2 * WP), 2 * WP), :] = jnp.concatenate(
            rows, axis=0
        ).astype(BF16)

    @pl.loop(0, TOKENS // 256, unroll=3)
    def _(m):
        rows = pl.ds(pl.multiple_of(m * 256, 256), 256)
        change = jnp.dot(mixed_rows[rows, :], proj_weight[...], preferred_element_type=F32)
        updated = (change + tokens[rows, :].astype(F32)).astype(BF16).astype(F32)
        mixed_rows[rows, :] = layer_norm(updated, out_gain_ref[...]).astype(BF16)

    copies[5].wait()

    @pl.loop(0, 2)
    def _(n):
        cols = pl.ds(pl.multiple_of(n * D, D), D)

        @pl.loop(0, 3, unroll=3)
        def _(m):
            rows = pl.ds(pl.multiple_of(m * 256, 256), 256)
            quad = jnp.dot(
                mixed_rows[rows, :], unembed_weight[:, cols], preferred_element_type=F32
            ).astype(BF16)
            for k in range(4):
                cells = jnp.dot(
                    quad[:, k * COLS : (k + 1) * COLS], read_pair[...], preferred_element_type=F32
                )
                pair = jnp.concatenate(
                    [cells[:, :CH].reshape(32, 8, CH), cells[:, CH:].reshape(32, 8, CH)], axis=1
                ).astype(BF16)
                place_at = pl.multiple_of(n * 64 + k * 16, 16)
                decoded[pl.ds(m * 32, 32), pl.ds(place_at, 16), :] = pair

    cell_iota = lax.broadcasted_iota(jnp.int32, (TILE, TILE), 0)

    @pl.loop(0, BLOCKS // GROUP)
    def _(part):
        for b in range(GROUP):
            block = part * GROUP + b
            cells = cells_ref[pl.ds(block, 1), :]
            one_hot = jnp.where(cell_iota == cells, 1.0, 0.0).astype(BF16)
            out_ref[block] = lax.dot_general(
                one_hot, decoded[tiles_ref[block]], (((0,), (0,)), ((), ())), preferred_element_type=F32
            ).astype(BF16)


def tail(meta, block_tiles, live_cells, tokens, sides, mixed_parts, out_gain, read_weight, qkv_weight, proj_weight, unembed_weight):
    return pl.pallas_call(
        tail_kernel,
        in_specs=[SMEM_SPEC, SMEM_SPEC] + [VMEM_SPEC, HBM_SPEC] + [VMEM_SPEC] * 8 + [HBM_SPEC] * 2 + [VMEM_SPEC] * 2 + [HBM_SPEC] * 3,
        out_specs=VMEM_SPEC,
        out_shape=pltpu.VMEM((BLOCKS, TILE, CH), BF16),
        scratch_shapes=attend_scratch(SIDES)
        + [
            pltpu.VMEM((SPAN_R, SPAN_C, D), F32),
            pltpu.VMEM((TOKENS, D), BF16),
            pltpu.VMEM((TOKENS, D), BF16),
            pltpu.VMEM((TILES, TILE, CH), BF16),
            pltpu.VMEM((2 * CH, 2 * CH), BF16),
            pltpu.VMEM((D, D), BF16),
            pltpu.VMEM((D, 2 * D), BF16),
            pltpu.SemaphoreType.DMA((6,)),
        ],
        compiler_params=pltpu.CompilerParams(vmem_limit_bytes=40 * MIB),
        cost_estimate=pl.CostEstimate(flops=12 * 10**9, bytes_accessed=28 * 10**6, transcendentals=10**6),
        name="sides_decode",
    )(
        meta, block_tiles, live_cells, in_hbm(tokens), *sides, *mixed_parts,
        out_gain, read_weight, in_hbm(qkv_weight), in_hbm(proj_weight), in_hbm(unembed_weight),
    )


def send(value, lon_step, lat_step):
    lon, lat = lax.axis_size("lon"), lax.axis_size("lat")
    pairs = [
        (i * lat + j, (i + lon_step) % lon * lat + (j + lat_step) % lat) for i in range(lon) for j in range(lat)
    ]
    return lax.ppermute(value, ("lon", "lat"), pairs)


def attention_and_decode(meta, block_tiles, live_cells, tokens, normed, west, east, north, south, out_gain, read_weight, qkv_weight, proj_weight, unembed_weight):
    from_north, from_south = send(south, 0, 1), send(north, 0, -1)
    from_west, from_east = send(east, 1, 0), send(west, -1, 0)
    inner = attend_windows(INNER, "inner_windows", meta, (in_hbm(normed),), qkv_weight)
    from_north, from_south, from_west, from_east, inner = lax.optimization_barrier(
        (from_north, from_south, from_west, from_east, inner)
    )
    first, last = slice(0, WIN_TOK), slice(2 * WIN_TOK, 3 * WIN_TOK)
    own_west = jnp.concatenate([from_north[first], from_south[first]], axis=0)
    own_east = jnp.concatenate([from_north[last], from_south[last]], axis=0)
    west_corners, east_corners = send(own_east, 1, 0), send(own_west, -1, 0)
    edges = attend_windows(EDGES, "edge_windows", meta, (from_north, north, south, from_south), qkv_weight)
    west_corners, east_corners, edges = lax.optimization_barrier((west_corners, east_corners, edges))
    sides = (west, east, from_west, from_east, own_west, own_east, west_corners, east_corners)
    return tail(
        meta, block_tiles, live_cells, tokens, sides, (inner, edges),
        out_gain, read_weight, qkv_weight, proj_weight, unembed_weight,
    )


def per_device(
    obs_values,
    obs_weights,
    block_counts,
    obs_cells,
    block_tiles,
    shift_offsets,
    embed_weight,
    patch_weight,
    norm_gain,
    qkv_weight,
    proj_weight,
    out_gain,
    unembed_weight,
    read_weight,
):
    outgoing = embed(
        block_counts.reshape(BLOCKS), obs_values.reshape(BLOCKS, TILE, CH), obs_weights.reshape(BLOCKS, TILE), embed_weight
    ).reshape(BLOCKS, 1, TILE, CH)
    received = lax.all_to_all(outgoing, ("lon", "lat"), split_axis=0, concat_axis=0, tiled=True)
    block_tiles = block_tiles.reshape(BLOCKS)
    tokens, normed, west, east, north, south, live_cells = grid_tokens(
        block_tiles, obs_cells.reshape(BLOCKS, TILE), norm_gain.reshape(1, D),
        received.reshape(BLOCKS, TILE, CH), patch_weight,
    )
    lat_index = lax.axis_index("lat")
    last = lax.axis_size("lat") - 1
    special = jnp.where(lat_index == 0, 0, jnp.where(lat_index == last, 4, -1)).astype(jnp.int32)
    meta = jnp.concatenate([shift_offsets, special.reshape(1)])
    sampled = attention_and_decode(
        meta, block_tiles, live_cells, tokens, normed, west, east, north, south,
        out_gain.reshape(1, D), read_weight, qkv_weight, proj_weight, unembed_weight,
    )
    returned = lax.all_to_all(
        sampled.reshape(BLOCKS, 1, TILE, CH), ("lon", "lat"), split_axis=0, concat_axis=0, tiled=True
    )
    return returned


def solution(mesh):
    rows = ("lon", "lat")
    in_specs = (
        P(rows, None, None, None),
        P(rows, None, None),
        P(rows, None),
        P(rows, None, None),
        P(rows, None),
    ) + (P(),) * 9
    out_specs = P(rows, None, None, None)
    return jax.shard_map(
        per_device, mesh=mesh, in_specs=in_specs, out_specs=out_specs, check_vma=False
    )
```

```python
import jax
import jax.numpy as jnp
from jax import lax
from jax.experimental import pallas as pl
from jax.experimental.pallas import tpu as pltpu
from jax.sharding import PartitionSpec as P

CH = 128
D = 1024
HEAD = 32
CELLS = 16
WIN = 8
TILE = 128
HP = 32
WP = 24
TILES = 96
TOKENS = HP * WP
BLOCKS = 128
GROUP = 16
SPAN_R = HP + WIN
SPAN_C = WP + WIN
EXT_R = HP + 2 * WIN
WIN_TOK = WIN * WIN
LANES = 128
COLS = 256
DEAD = 1e30
GELU = 0.7978845608028654
EXCLUDED = -1e9 * HEAD**0.5
EXP_SCALE = 1.4426950408889634 * HEAD**-0.5
DEAD_LIMIT = 1e6
MIB = 1024 * 1024
F32 = jnp.float32
BF16 = jnp.bfloat16


VMEM_SPEC = pl.BlockSpec(memory_space=pltpu.VMEM)
SMEM_SPEC = pl.BlockSpec(memory_space=pltpu.SMEM)
HBM_SPEC = pl.BlockSpec(memory_space=pl.ANY)


def in_hbm(value):
    return pltpu.with_memory_space_constraint(value, pltpu.HBM)


def in_vmem(value):
    return pltpu.with_memory_space_constraint(value, pltpu.VMEM)


def layer_norm(values, gain_vector):
    row_mean = jnp.mean(values, axis=-1, keepdims=True)
    centered = values - row_mean
    variance = jnp.mean(centered * centered, axis=-1, keepdims=True)
    return centered * lax.rsqrt(variance + 1e-05) * gain_vector


def embed_kernel(counts_ref, weights_ref, embed_ref, values_hbm, out, values, in_sems):
    parts = BLOCKS // GROUP

    def arrival(part):
        rows = pl.ds(part * GROUP, GROUP)
        return pltpu.make_async_copy(values_hbm.at[rows], values.at[rows], in_sems.at[part])

    for part in range(parts):
        arrival(part).start()
    slot_iota = lax.broadcasted_iota(jnp.int32, (TILE, CH), 0)

    @pl.loop(0, parts, unroll=4)
    def _(part):
        first = pl.multiple_of(part * GROUP, GROUP)
        columns = (weights_ref[pl.ds(first, GROUP), :] * 0.5).T
        arrival(part).wait()
        for b in range(GROUP):
            raw = jnp.dot(values[first + b], embed_ref[...], preferred_element_type=F32)
            inner = jnp.tanh(raw * (GELU + GELU * 0.044715 * (raw * raw)))
            embedded = raw * columns[:, b : b + 1] * (1.0 + inner)
            out[first + b] = jnp.where(slot_iota < counts_ref[first + b], embedded, DEAD).astype(BF16)


def embed(block_counts, obs_values, obs_weights, embed_weight):
    return pl.pallas_call(
        embed_kernel,
        in_specs=[SMEM_SPEC, VMEM_SPEC, VMEM_SPEC, HBM_SPEC],
        out_specs=VMEM_SPEC,
        out_shape=pltpu.VMEM((BLOCKS, TILE, CH), BF16),
        scratch_shapes=[
            pltpu.VMEM((BLOCKS, TILE, CH), BF16),
            pltpu.SemaphoreType.DMA((BLOCKS // GROUP,)),
        ],
        compiler_params=pltpu.CompilerParams(vmem_limit_bytes=24 * MIB),
        cost_estimate=pl.CostEstimate(flops=6 * 10**8, bytes_accessed=8 * 10**6, transcendentals=2 * 10**6),
        name="embed",
    )(in_hbm(block_counts), in_hbm(obs_weights), in_hbm(embed_weight), in_hbm(obs_values))


def grid_kernel(
    tiles_ref, cells_ref, gain_ref, received, patch_hbm,
    tokens_hbm, normed_hbm, west_ref, east_ref, north_ref, south_ref, live_cells_ref,
    cell_sums, patch_rows, patch_weight, tokens, normed, weight_sem, out_sems,
):
    parts = BLOCKS // GROUP
    weight_copy = pltpu.make_async_copy(patch_hbm, patch_weight, weight_sem)
    weight_copy.start()

    @pl.loop(0, TILES, unroll=2)
    def _(tile):
        cell_sums[tile] = jnp.zeros((TILE, CH), F32)

    cell_iota = lax.broadcasted_iota(jnp.int32, (TILE, TILE), 0)
    slot_iota = lax.broadcasted_iota(jnp.int32, (1, TILE), 1).astype(F32)

    @pl.loop(0, parts, unroll=4)
    def _(part):
        first = pl.multiple_of(part * GROUP, GROUP)
        all_cells = cells_ref[pl.ds(first, GROUP), :]
        all_cells = (all_cells & 15) * 8 + (all_cells >> 4)
        live_rows = []
        for b in range(GROUP):
            cells = all_cells[b : b + 1, :]
            block = received[first + b]
            live = block < jnp.asarray(DEAD_LIMIT, BF16)
            block = jnp.where(live, block, jnp.zeros_like(block))
            count = jnp.sum(jnp.where(live, 1.0, 0.0).astype(F32), axis=0, keepdims=True)
            live_rows.append(jnp.where(slot_iota < count, cells, -1))
            one_hot = jnp.where(cell_iota == cells, 1.0, 0.0).astype(BF16)
            tile = tiles_ref[first + b]
            cell_sums[tile] += jnp.dot(one_hot, block, preferred_element_type=F32)
        live_cells_ref[pl.ds(first, GROUP), :] = jnp.concatenate(live_rows, axis=0)

    weight_copy.wait()
    half_rows = HP // 2
    block = half_rows * WP

    def leave(m):
        rows = pl.ds(m * block, block)
        return (
            pltpu.make_async_copy(tokens.at[rows], tokens_hbm.at[rows], out_sems.at[2 * m]),
            pltpu.make_async_copy(normed.at[rows], normed_hbm.at[rows], out_sems.at[2 * m + 1]),
        )

    for m in range(2):
        rows = slice(m * block, (m + 1) * block)
        tiles = cell_sums[m * (TILES // 2) : (m + 1) * (TILES // 2)].reshape(TILES // 2, CELLS, 8, CH)
        for cell in range(CELLS):
            patch_rows[rows, cell * CH : (cell + 1) * CH] = tiles[:, cell].reshape(block, CH).astype(BF16)
        part = jnp.dot(patch_rows[rows, :], patch_weight[...], preferred_element_type=F32).astype(BF16)
        tokens[rows, :] = part
        values = layer_norm(part.astype(F32), gain_ref[...])
        normed[rows, :] = values.astype(BF16)
        values = values.reshape(half_rows, 3, WIN, D)
        side = slice(m * half_rows * WIN, (m + 1) * half_rows * WIN)
        west_ref[side, :] = values[:, 0].reshape(half_rows * WIN, D).astype(BF16)
        east_ref[side, :] = values[:, 2].reshape(half_rows * WIN, D).astype(BF16)
        ends, target = (values[:WIN], north_ref) if m == 0 else (values[half_rows - WIN :], south_ref)
        for col in range(3):
            target[col * WIN_TOK : (col + 1) * WIN_TOK, :] = ends[:, col].reshape(WIN_TOK, D).astype(BF16)
        for copy in leave(m):
            copy.start()

    for m in range(2):
        for copy in leave(m):
            copy.wait()


def grid_tokens(block_tiles, obs_cells, norm_gain, received, patch_weight):
    whole = lambda rows: jax.ShapeDtypeStruct((rows, D), BF16)
    outs = [pltpu.HBM((TOKENS, D), BF16)] * 2 + [whole(n) for n in (WIN * HP, WIN * HP, WIN * WP, WIN * WP)]
    outs.append(jax.ShapeDtypeStruct((BLOCKS, TILE), jnp.int32))
    return pl.pallas_call(
        grid_kernel,
        in_specs=[SMEM_SPEC, VMEM_SPEC, VMEM_SPEC, VMEM_SPEC, HBM_SPEC],
        out_specs=[HBM_SPEC] * 2 + [VMEM_SPEC] * (len(outs) - 2),
        scratch_shapes=[
            pltpu.VMEM((TILES, TILE, CH), F32),
            pltpu.VMEM((TOKENS, CELLS * CH), BF16),
            pltpu.VMEM((CELLS * CH, D), BF16),
            pltpu.VMEM((TOKENS, D), BF16),
            pltpu.VMEM((TOKENS, D), BF16),
            pltpu.SemaphoreType.DMA,
            pltpu.SemaphoreType.DMA((4,)),
        ],
        out_shape=outs,
        compiler_params=pltpu.CompilerParams(vmem_limit_bytes=32 * MIB),
        cost_estimate=pl.CostEstimate(flops=4 * 10**9, bytes_accessed=14 * 10**6, transcendentals=0),
        name="grid_tokens",
    )(block_tiles, obs_cells, norm_gain, in_vmem(received), in_hbm(patch_weight))


INNER = (1, 1, 3, (1, 2))
EDGES = (0, 4, 2, (1, 2))
SIDES = (0, 1, 5, (0, 3))


def slots_of(windows):
    return windows[2] * len(windows[3])


def place(source, first, ext, across, rows, row, col, width):
    @pl.loop(0, rows // 2, unroll=2)
    def _(pair):
        both = source[pl.ds(pl.multiple_of(first + pair * 2 * width, 16), 2 * width), :].astype(F32)
        at = (row + pair * 2) * across + col
        ext[pl.ds(pl.multiple_of(at, 8), width), :] = both[:width]
        ext[pl.ds(pl.multiple_of(at + across, 8), width), :] = both[width:]


def attend(windows, meta_ref, ext, qkv_hbm, picked, qkv, qkv_weight, bias, ones, weight_sems, fill, store, later=None):
    row_shift, col_shift, special = meta_ref[0], meta_ref[1], meta_ref[2]
    first, stride, count, cols = windows
    total = slots_of(windows) * WIN_TOK

    def weights(part):
        cols = pl.ds(pl.multiple_of(part * D, D), D)
        return pltpu.make_async_copy(qkv_hbm.at[:, cols], qkv_weight.at[:, cols], weight_sems.at[part])

    for part in range(3):
        weights(part).start()
    ones[...] = (
        lax.broadcasted_iota(jnp.int32, (4 * WIN_TOK, LANES), 0) // WIN_TOK
        == lax.broadcasted_iota(jnp.int32, (4 * WIN_TOK, LANES), 1) // HEAD
    ).astype(F32).astype(BF16)
    row_step = fill()

    @pl.loop(0, count * 4, unroll=2)
    def _(pair):
        step, quarter = pair // 4, pair % 4
        row = row_step * step + quarter * 2 + row_shift
        for index, col in enumerate(cols):
            rows = []
            for half in range(2):
                if windows is SIDES:
                    at = pl.multiple_of((row + half) * 4 * WIN + index * 2 * WIN, 2 * WIN)
                    rows.append(pltpu.roll(ext[pl.ds(at, 2 * WIN), :], 2 * WIN - col_shift, 0)[:WIN])
                else:
                    at = pl.multiple_of((row + half) * WP, 8)
                    around = pltpu.roll(ext[pl.ds(at, WP), :], WP - col_shift, 0)
                    rows.append(around[index * WIN : (index + 1) * WIN])
            at = (step * len(cols) + index) * WIN_TOK + quarter * 16
            picked[pl.ds(pl.multiple_of(at, 16), 16), :] = jnp.concatenate(rows, axis=0).astype(BF16)

    block = total // 2 if total > 512 else total

    @pl.loop(0, 3)
    def _(n):
        weights(n).wait()
        lanes = pl.ds(pl.multiple_of(n * D, D), D)

        @pl.loop(0, total // block, unroll=total // block)
        def _(m):
            rows = pl.ds(pl.multiple_of(m * block, block), block)
            qkv[rows, lanes] = jnp.dot(
                picked[rows, :], qkv_weight[:, lanes], preferred_element_type=F32
            ).astype(BF16)

    if later is not None:
        later()
    edge_rows = first == 0
    if edge_rows:

        @pl.loop(0, WIN)
        def _(i):
            query_flag = jnp.where(i >= WIN - row_shift, 1, 0)
            key_row = (lax.broadcasted_iota(jnp.int32, (WIN, LANES), 1) % WIN_TOK) // WIN
            key_flag = jnp.where(key_row >= WIN - row_shift, 1, 0)
            bias[1, pl.ds(pl.multiple_of(i * WIN, 8), WIN), :] = jnp.where(key_flag == query_flag, 0.0, 1.0)

        bias[0] = jnp.zeros((WIN_TOK, LANES), F32)

    for step in range(count):
        row = first + stride * step
        mask = bias.at[jnp.where(row == special, 1, 0)] if row in (0, 4) else None

        @pl.loop(0, D // LANES, unroll=8)
        def _(group, step=step, mask=mask):
            for index in range(len(cols)):
                result = attention_group(qkv, mask, ones, step * len(cols) + index, group)
                lanes = pl.ds(pl.multiple_of(group * LANES, LANES), LANES)
                for i in range(WIN):
                    store(step, index, i, lanes, result[i * WIN : (i + 1) * WIN])


def attention_group(qkv, mask, ones, slot, group):
    rows = pl.ds(pl.multiple_of(slot * WIN_TOK, WIN_TOK), WIN_TOK)
    lanes = lambda part: pl.ds(pl.multiple_of(part * D + group * LANES, LANES), LANES)
    query, key, value = (qkv[rows, lanes(part)] for part in range(3))
    head_of_lane = lax.broadcasted_iota(jnp.int32, (WIN_TOK, LANES), 1) // HEAD
    zero = jnp.zeros((WIN_TOK, LANES), BF16)
    spread = lambda x: jnp.concatenate([jnp.where(head_of_lane == h, x, zero) for h in range(4)], axis=0)
    scores = lax.dot_general(query, spread(key), (((1,), (1,)), ((), ())), preferred_element_type=F32)
    low = lax.broadcasted_iota(jnp.int32, (WIN_TOK, LANES), 1) < WIN_TOK
    parts = []
    for half in range(2):
        part = scores[:, half * LANES : (half + 1) * LANES]
        if mask is not None:
            part = jnp.where(mask[...] < 0.5, part, EXCLUDED)
        low_max = jnp.max(jnp.where(low, part, -jnp.inf), axis=-1, keepdims=True)
        high_max = jnp.max(jnp.where(low, -jnp.inf, part), axis=-1, keepdims=True)
        parts.append(jnp.exp2((part - jnp.where(low, low_max, high_max)) * EXP_SCALE).astype(BF16))
    weights = jnp.concatenate(parts, axis=1)
    both = jnp.dot(weights, jnp.concatenate([spread(value), ones[...]], axis=1), preferred_element_type=F32)
    total = both[:, LANES:]
    inverse = pl.reciprocal(total, approx=True)
    inverse = inverse * (2.0 - total * inverse)
    return (both[:, :LANES] * inverse).astype(BF16).astype(F32)


def windows_kernel(windows, *refs):
    meta_ref, *sources, qkv_hbm, out, ext, picked, qkv, qkv_weight, bias, ones, weight_sems = refs

    def fill():
        if windows is INNER:
            place(sources[0], 0, ext, WP, HP, 0, 0, WP)
            return WIN
        for index, source in enumerate(sources):
            for col in range(3):
                place(source, col * WIN_TOK, ext, WP, WIN, index * WIN, col * WIN, WIN)
        return 2 * WIN

    def store(step, index, i, lanes, value):
        out[step * WIN + i, index * WIN : (index + 1) * WIN, lanes] = value

    attend(windows, meta_ref, ext, qkv_hbm, picked, qkv, qkv_weight, bias, ones, weight_sems, fill, store)


def attend_scratch(windows):
    rows = slots_of(windows) * WIN_TOK
    return [
        pltpu.VMEM((EXT_R * 4 * WIN if windows is SIDES else HP * WP, D), F32),
        pltpu.VMEM((rows, D), BF16),
        pltpu.VMEM((rows, 3 * D), BF16),
        pltpu.VMEM((D, 3 * D), BF16),
        pltpu.VMEM((2, WIN_TOK, LANES), F32),
        pltpu.VMEM((4 * WIN_TOK, LANES), BF16),
        pltpu.SemaphoreType.DMA((3,)),
    ]


def attend_windows(windows, name, meta, sources, qkv_weight):
    rows = slots_of(windows) * WIN_TOK
    return pl.pallas_call(
        lambda *refs: windows_kernel(windows, *refs),
        in_specs=[SMEM_SPEC] + [VMEM_SPEC] * len(sources) + [HBM_SPEC],
        out_specs=VMEM_SPEC,
        out_shape=jax.ShapeDtypeStruct((windows[2] * WIN, 2 * WIN, D), F32),
        scratch_shapes=attend_scratch(windows),
        compiler_params=pltpu.CompilerParams(vmem_limit_bytes=28 * MIB),
        cost_estimate=pl.CostEstimate(
            flops=rows * D * 3 * D * 3, bytes_accessed=12 * 10**6, transcendentals=rows * 2048
        ),
        name=name,
    )(meta, *sources, in_hbm(qkv_weight))


def tail_kernel(
    meta_ref, tiles_ref, cells_ref, tokens_hbm,
    west_ref, east_ref, from_west_ref, from_east_ref, own_west_ref, own_east_ref, west_corners_ref, east_corners_ref,
    inner_hbm, edges_hbm, out_gain_ref, read_ref, qkv_hbm, proj_hbm, unembed_hbm,
    out_ref,
    ext, picked, qkv, qkv_weight, bias, ones, weight_sems,
    mixed, mixed_rows, tokens, decoded, read_pair,
    proj_weight, unembed_weight, in_sems,
):
    row_shift, col_shift = meta_ref[0], meta_ref[1]
    inner_cols = pl.ds(WIN, 2 * WIN)
    moves = (
        (inner_hbm, mixed.at[pl.ds(WIN, 3 * WIN), inner_cols, :]),
        (edges_hbm.at[pl.ds(0, WIN)], mixed.at[pl.ds(0, WIN), inner_cols, :]),
        (edges_hbm.at[pl.ds(WIN, WIN)], mixed.at[pl.ds(SPAN_R - WIN, WIN), inner_cols, :]),
        (proj_hbm, proj_weight),
        (tokens_hbm, tokens),
        (unembed_hbm, unembed_weight),
    )
    copies = [pltpu.make_async_copy(src, dst, in_sems.at[i]) for i, (src, dst) in enumerate(moves)]

    def fill():
        columns = (
            (from_west_ref, west_corners_ref), (west_ref, own_west_ref),
            (east_ref, own_east_ref), (from_east_ref, east_corners_ref),
        )
        for index, (middle, ends) in enumerate(columns):
            place(middle, 0, ext, 4 * WIN, HP, WIN, index * WIN, WIN)
            place(ends, 0, ext, 4 * WIN, WIN, 0, index * WIN, WIN)
            place(ends, WIN_TOK, ext, 4 * WIN, WIN, WIN + HP, index * WIN, WIN)
        read_pair[...] = jnp.zeros((2 * CH, 2 * CH), BF16)
        read_pair[:CH, :CH] = read_ref[...]
        read_pair[CH:, CH:] = read_ref[...]
        return WIN

    def store(step, index, i, lanes, value):
        mixed[step * WIN + i, index * 3 * WIN : index * 3 * WIN + WIN, lanes] = value

    def later():
        for copy in copies:
            copy.start()

    attend(SIDES, meta_ref, ext, qkv_hbm, picked, qkv, qkv_weight, bias, ones, weight_sems, fill, store, later)
    for copy in copies[:5]:
        copy.wait()

    @pl.loop(0, HP // 2, unroll=2)
    def _(pair):
        rows = [
            pltpu.roll(mixed[WIN - row_shift + pair * 2 + half], SPAN_C - WIN + col_shift, 0)[:WP]
            for half in range(2)
        ]
        mixed_rows[pl.ds(pl.multiple_of(pair * 2 * WP, 2 * WP), 2 * WP), :] = jnp.concatenate(
            rows, axis=0
        ).astype(BF16)

    @pl.loop(0, TOKENS // 256, unroll=3)
    def _(m):
        rows = pl.ds(pl.multiple_of(m * 256, 256), 256)
        change = jnp.dot(mixed_rows[rows, :], proj_weight[...], preferred_element_type=F32)
        updated = (change + tokens[rows, :].astype(F32)).astype(BF16).astype(F32)
        mixed_rows[rows, :] = layer_norm(updated, out_gain_ref[...]).astype(BF16)

    copies[5].wait()

    @pl.loop(0, 2)
    def _(n):
        cols = pl.ds(pl.multiple_of(n * D, D), D)

        @pl.loop(0, 3, unroll=3)
        def _(m):
            rows = pl.ds(pl.multiple_of(m * 256, 256), 256)
            quad = jnp.dot(
                mixed_rows[rows, :], unembed_weight[:, cols], preferred_element_type=F32
            ).astype(BF16)
            for k in range(4):
                cells = jnp.dot(
                    quad[:, k * COLS : (k + 1) * COLS], read_pair[...], preferred_element_type=F32
                )
                pair = jnp.concatenate(
                    [cells[:, :CH].reshape(32, 8, CH), cells[:, CH:].reshape(32, 8, CH)], axis=1
                ).astype(BF16)
                place_at = pl.multiple_of(n * 64 + k * 16, 16)
                decoded[pl.ds(m * 32, 32), pl.ds(place_at, 16), :] = pair

    cell_iota = lax.broadcasted_iota(jnp.int32, (TILE, TILE), 0)

    @pl.loop(0, BLOCKS // GROUP, unroll=2)
    def _(part):
        for b in range(GROUP):
            block = part * GROUP + b
            cells = cells_ref[pl.ds(block, 1), :]
            one_hot = jnp.where(cell_iota == cells, 1.0, 0.0).astype(BF16)
            out_ref[block] = lax.dot_general(
                one_hot, decoded[tiles_ref[block]], (((0,), (0,)), ((), ())), preferred_element_type=F32
            ).astype(BF16)


def tail(meta, block_tiles, live_cells, tokens, sides, mixed_parts, out_gain, read_weight, qkv_weight, proj_weight, unembed_weight):
    return pl.pallas_call(
        tail_kernel,
        in_specs=[SMEM_SPEC, SMEM_SPEC] + [VMEM_SPEC, HBM_SPEC] + [VMEM_SPEC] * 8 + [HBM_SPEC] * 2 + [VMEM_SPEC] * 2 + [HBM_SPEC] * 3,
        out_specs=VMEM_SPEC,
        out_shape=pltpu.VMEM((BLOCKS, TILE, CH), BF16),
        scratch_shapes=attend_scratch(SIDES)
        + [
            pltpu.VMEM((SPAN_R, SPAN_C, D), F32),
            pltpu.VMEM((TOKENS, D), BF16),
            pltpu.VMEM((TOKENS, D), BF16),
            pltpu.VMEM((TILES, TILE, CH), BF16),
            pltpu.VMEM((2 * CH, 2 * CH), BF16),
            pltpu.VMEM((D, D), BF16),
            pltpu.VMEM((D, 2 * D), BF16),
            pltpu.SemaphoreType.DMA((6,)),
        ],
        compiler_params=pltpu.CompilerParams(vmem_limit_bytes=40 * MIB),
        cost_estimate=pl.CostEstimate(flops=12 * 10**9, bytes_accessed=28 * 10**6, transcendentals=10**6),
        name="sides_decode",
    )(
        meta, block_tiles, live_cells, in_hbm(tokens), *sides, *mixed_parts,
        out_gain, read_weight, in_hbm(qkv_weight), in_hbm(proj_weight), in_hbm(unembed_weight),
    )


def send(value, lon_step, lat_step):
    lon, lat = lax.axis_size("lon"), lax.axis_size("lat")
    pairs = [
        (i * lat + j, (i + lon_step) % lon * lat + (j + lat_step) % lat) for i in range(lon) for j in range(lat)
    ]
    return lax.ppermute(value, ("lon", "lat"), pairs)


def attention_and_decode(meta, block_tiles, live_cells, tokens, normed, west, east, north, south, out_gain, read_weight, qkv_weight, proj_weight, unembed_weight):
    from_north, from_south = send(south, 0, 1), send(north, 0, -1)
    from_west, from_east = send(east, 1, 0), send(west, -1, 0)
    inner = attend_windows(INNER, "inner_windows", meta, (in_hbm(normed),), qkv_weight)
    from_north, from_south, from_west, from_east, inner = lax.optimization_barrier(
        (from_north, from_south, from_west, from_east, inner)
    )
    first, last = slice(0, WIN_TOK), slice(2 * WIN_TOK, 3 * WIN_TOK)
    own_west = jnp.concatenate([from_north[first], from_south[first]], axis=0)
    own_east = jnp.concatenate([from_north[last], from_south[last]], axis=0)
    west_corners, east_corners = send(own_east, 1, 0), send(own_west, -1, 0)
    edges = attend_windows(EDGES, "edge_windows", meta, (from_north, north, south, from_south), qkv_weight)
    west_corners, east_corners, edges = lax.optimization_barrier((west_corners, east_corners, edges))
    sides = (west, east, from_west, from_east, own_west, own_east, west_corners, east_corners)
    return tail(
        meta, block_tiles, live_cells, tokens, sides, (inner, edges),
        out_gain, read_weight, qkv_weight, proj_weight, unembed_weight,
    )


def per_device(
    obs_values,
    obs_weights,
    block_counts,
    obs_cells,
    block_tiles,
    shift_offsets,
    embed_weight,
    patch_weight,
    norm_gain,
    qkv_weight,
    proj_weight,
    out_gain,
    unembed_weight,
    read_weight,
):
    outgoing = embed(
        block_counts.reshape(BLOCKS), obs_values.reshape(BLOCKS, TILE, CH), obs_weights.reshape(BLOCKS, TILE), embed_weight
    ).reshape(BLOCKS, 1, TILE, CH)
    received = lax.all_to_all(outgoing, ("lon", "lat"), split_axis=0, concat_axis=0, tiled=True)
    block_tiles = block_tiles.reshape(BLOCKS)
    tokens, normed, west, east, north, south, live_cells = grid_tokens(
        block_tiles, obs_cells.reshape(BLOCKS, TILE), norm_gain.reshape(1, D),
        received.reshape(BLOCKS, TILE, CH), patch_weight,
    )
    lat_index = lax.axis_index("lat")
    last = lax.axis_size("lat") - 1
    special = jnp.where(lat_index == 0, 0, jnp.where(lat_index == last, 4, -1)).astype(jnp.int32)
    meta = jnp.concatenate([shift_offsets, special.reshape(1)])
    sampled = attention_and_decode(
        meta, block_tiles, live_cells, tokens, normed, west, east, north, south,
        out_gain.reshape(1, D), read_weight, qkv_weight, proj_weight, unembed_weight,
    )
    returned = lax.all_to_all(
        sampled.reshape(BLOCKS, 1, TILE, CH), ("lon", "lat"), split_axis=0, concat_axis=0, tiled=True
    )
    return returned


def solution(mesh):
    rows = ("lon", "lat")
    in_specs = (
        P(rows, None, None, None),
        P(rows, None, None),
        P(rows, None),
        P(rows, None, None),
        P(rows, None),
    ) + (P(),) * 9
    out_specs = P(rows, None, None, None)
    return jax.shard_map(
        per_device, mesh=mesh, in_specs=in_specs, out_specs=out_specs, check_vma=False
    )
```

```python
import jax
import jax.numpy as jnp
from jax import lax
from jax.experimental import pallas as pl
from jax.experimental.pallas import tpu as pltpu
from jax.sharding import PartitionSpec as P

CH = 128
D = 1024
HEAD = 32
CELLS = 16
WIN = 8
TILE = 128
HP = 32
WP = 24
TILES = 96
TOKENS = HP * WP
BLOCKS = 128
GROUP = 16
SPAN_R = HP + WIN
SPAN_C = WP + WIN
EXT_R = HP + 2 * WIN
WIN_TOK = WIN * WIN
LANES = 128
COLS = 256
DEAD = 1e30
GELU = 0.7978845608028654
EXCLUDED = -1e9 * HEAD**0.5
EXP_SCALE = 1.4426950408889634 * HEAD**-0.5
DEAD_LIMIT = 1e6
MIB = 1024 * 1024
F32 = jnp.float32
BF16 = jnp.bfloat16


VMEM_SPEC = pl.BlockSpec(memory_space=pltpu.VMEM)
SMEM_SPEC = pl.BlockSpec(memory_space=pltpu.SMEM)
HBM_SPEC = pl.BlockSpec(memory_space=pl.ANY)


def in_hbm(value):
    return pltpu.with_memory_space_constraint(value, pltpu.HBM)


def in_vmem(value):
    return pltpu.with_memory_space_constraint(value, pltpu.VMEM)


def layer_norm(values, gain_vector):
    row_mean = jnp.mean(values, axis=-1, keepdims=True)
    centered = values - row_mean
    variance = jnp.mean(centered * centered, axis=-1, keepdims=True)
    return centered * lax.rsqrt(variance + 1e-05) * gain_vector


def embed_kernel(counts_ref, weights_ref, embed_ref, values_hbm, out, values, in_sems):
    parts = BLOCKS // GROUP

    def arrival(part):
        rows = pl.ds(part * GROUP, GROUP)
        return pltpu.make_async_copy(values_hbm.at[rows], values.at[rows], in_sems.at[part])

    for part in range(parts):
        arrival(part).start()
    slot_iota = lax.broadcasted_iota(jnp.int32, (TILE, CH), 0)

    @pl.loop(0, parts, unroll=4)
    def _(part):
        first = pl.multiple_of(part * GROUP, GROUP)
        columns = (weights_ref[pl.ds(first, GROUP), :] * 0.5).T
        arrival(part).wait()
        for b in range(GROUP):
            raw = jnp.dot(values[first + b], embed_ref[...], preferred_element_type=F32)
            inner = jnp.tanh(raw * (GELU + GELU * 0.044715 * (raw * raw)))
            embedded = raw * columns[:, b : b + 1] * (1.0 + inner)
            out[first + b] = jnp.where(slot_iota < counts_ref[first + b], embedded, DEAD).astype(BF16)


def embed(block_counts, obs_values, obs_weights, embed_weight):
    return pl.pallas_call(
        embed_kernel,
        in_specs=[SMEM_SPEC, VMEM_SPEC, VMEM_SPEC, HBM_SPEC],
        out_specs=VMEM_SPEC,
        out_shape=pltpu.VMEM((BLOCKS, TILE, CH), BF16),
        scratch_shapes=[
            pltpu.VMEM((BLOCKS, TILE, CH), BF16),
            pltpu.SemaphoreType.DMA((BLOCKS // GROUP,)),
        ],
        compiler_params=pltpu.CompilerParams(vmem_limit_bytes=24 * MIB),
        cost_estimate=pl.CostEstimate(flops=6 * 10**8, bytes_accessed=8 * 10**6, transcendentals=2 * 10**6),
        name="embed",
    )(in_hbm(block_counts), in_hbm(obs_weights), in_hbm(embed_weight), in_hbm(obs_values))


def grid_kernel(
    tiles_ref, cells_ref, gain_ref, received, patch_hbm,
    tokens_hbm, normed_hbm, west_ref, east_ref, north_ref, south_ref, live_cells_ref,
    cell_sums, patch_rows, patch_weight, tokens, normed, weight_sem, out_sems,
):
    parts = BLOCKS // GROUP
    weight_copy = pltpu.make_async_copy(patch_hbm, patch_weight, weight_sem)
    weight_copy.start()

    @pl.loop(0, TILES, unroll=2)
    def _(tile):
        cell_sums[tile] = jnp.zeros((TILE, CH), F32)

    cell_iota = lax.broadcasted_iota(jnp.int32, (TILE, TILE), 0)
    slot_iota = lax.broadcasted_iota(jnp.int32, (1, TILE), 1).astype(F32)

    @pl.loop(0, parts, unroll=4)
    def _(part):
        first = pl.multiple_of(part * GROUP, GROUP)
        all_cells = cells_ref[pl.ds(first, GROUP), :]
        all_cells = (all_cells & 15) * 8 + (all_cells >> 4)
        live_rows = []
        for b in range(GROUP):
            cells = all_cells[b : b + 1, :]
            block = received[first + b]
            live = block < jnp.asarray(DEAD_LIMIT, BF16)
            block = jnp.where(live, block, jnp.zeros_like(block))
            count = jnp.sum(jnp.where(live, 1.0, 0.0).astype(F32), axis=0, keepdims=True)
            live_rows.append(jnp.where(slot_iota < count, cells, -1))
            one_hot = jnp.where(cell_iota == cells, 1.0, 0.0).astype(BF16)
            tile = tiles_ref[first + b]
            cell_sums[tile] += jnp.dot(one_hot, block, preferred_element_type=F32)
        live_cells_ref[pl.ds(first, GROUP), :] = jnp.concatenate(live_rows, axis=0)

    weight_copy.wait()
    half_rows = HP // 2
    block = half_rows * WP

    def leave(m):
        rows = pl.ds(m * block, block)
        return (
            pltpu.make_async_copy(tokens.at[rows], tokens_hbm.at[rows], out_sems.at[2 * m]),
            pltpu.make_async_copy(normed.at[rows], normed_hbm.at[rows], out_sems.at[2 * m + 1]),
        )

    for m in range(2):
        rows = slice(m * block, (m + 1) * block)
        tiles = cell_sums[m * (TILES // 2) : (m + 1) * (TILES // 2)].reshape(TILES // 2, CELLS, 8, CH)
        for cell in range(CELLS):
            patch_rows[rows, cell * CH : (cell + 1) * CH] = tiles[:, cell].reshape(block, CH).astype(BF16)
        part = jnp.dot(patch_rows[rows, :], patch_weight[...], preferred_element_type=F32).astype(BF16)
        tokens[rows, :] = part
        values = layer_norm(part.astype(F32), gain_ref[...])
        normed[rows, :] = values.astype(BF16)
        values = values.reshape(half_rows, 3, WIN, D)
        side = slice(m * half_rows * WIN, (m + 1) * half_rows * WIN)
        west_ref[side, :] = values[:, 0].reshape(half_rows * WIN, D).astype(BF16)
        east_ref[side, :] = values[:, 2].reshape(half_rows * WIN, D).astype(BF16)
        ends, target = (values[:WIN], north_ref) if m == 0 else (values[half_rows - WIN :], south_ref)
        for col in range(3):
            target[col * WIN_TOK : (col + 1) * WIN_TOK, :] = ends[:, col].reshape(WIN_TOK, D).astype(BF16)
        for copy in leave(m):
            copy.start()

    for m in range(2):
        for copy in leave(m):
            copy.wait()


def grid_tokens(block_tiles, obs_cells, norm_gain, received, patch_weight):
    whole = lambda rows: jax.ShapeDtypeStruct((rows, D), BF16)
    outs = [pltpu.HBM((TOKENS, D), BF16)] * 2 + [whole(n) for n in (WIN * HP, WIN * HP, WIN * WP, WIN * WP)]
    outs.append(jax.ShapeDtypeStruct((BLOCKS, TILE), jnp.int32))
    return pl.pallas_call(
        grid_kernel,
        in_specs=[SMEM_SPEC, VMEM_SPEC, VMEM_SPEC, VMEM_SPEC, HBM_SPEC],
        out_specs=[HBM_SPEC] * 2 + [VMEM_SPEC] * (len(outs) - 2),
        scratch_shapes=[
            pltpu.VMEM((TILES, TILE, CH), F32),
            pltpu.VMEM((TOKENS, CELLS * CH), BF16),
            pltpu.VMEM((CELLS * CH, D), BF16),
            pltpu.VMEM((TOKENS, D), BF16),
            pltpu.VMEM((TOKENS, D), BF16),
            pltpu.SemaphoreType.DMA,
            pltpu.SemaphoreType.DMA((4,)),
        ],
        out_shape=outs,
        compiler_params=pltpu.CompilerParams(vmem_limit_bytes=32 * MIB),
        cost_estimate=pl.CostEstimate(flops=4 * 10**9, bytes_accessed=14 * 10**6, transcendentals=0),
        name="grid_tokens",
    )(block_tiles, obs_cells, norm_gain, in_vmem(received), in_hbm(patch_weight))


INNER = (1, 1, 3, (1, 2))
EDGES = (0, 4, 2, (1, 2))
SIDES = (0, 1, 5, (0, 3))


def slots_of(windows):
    return windows[2] * len(windows[3])


def place(source, first, ext, across, rows, row, col, width):
    @pl.loop(0, rows // 2, unroll=2)
    def _(pair):
        both = source[pl.ds(pl.multiple_of(first + pair * 2 * width, 16), 2 * width), :].astype(F32)
        at = (row + pair * 2) * across + col
        ext[pl.ds(pl.multiple_of(at, 8), width), :] = both[:width]
        ext[pl.ds(pl.multiple_of(at + across, 8), width), :] = both[width:]


def attend(windows, meta_ref, ext, qkv_hbm, picked, qkv, qkv_weight, bias, ones, weight_sems, fill, store, later=None):
    row_shift, col_shift, special = meta_ref[0], meta_ref[1], meta_ref[2]
    first, stride, count, cols = windows
    total = slots_of(windows) * WIN_TOK

    def weights(part):
        cols = pl.ds(pl.multiple_of(part * D, D), D)
        return pltpu.make_async_copy(qkv_hbm.at[:, cols], qkv_weight.at[:, cols], weight_sems.at[part])

    for part in range(3):
        weights(part).start()
    ones[...] = (
        lax.broadcasted_iota(jnp.int32, (4 * WIN_TOK, LANES), 0) // WIN_TOK
        == lax.broadcasted_iota(jnp.int32, (4 * WIN_TOK, LANES), 1) // HEAD
    ).astype(F32).astype(BF16)
    row_step = fill()

    @pl.loop(0, count * 4, unroll=2)
    def _(pair):
        step, quarter = pair // 4, pair % 4
        row = row_step * step + quarter * 2 + row_shift
        for index, col in enumerate(cols):
            rows = []
            for half in range(2):
                if windows is SIDES:
                    at = pl.multiple_of((row + half) * 4 * WIN + index * 2 * WIN, 2 * WIN)
                    rows.append(pltpu.roll(ext[pl.ds(at, 2 * WIN), :], 2 * WIN - col_shift, 0)[:WIN])
                else:
                    at = pl.multiple_of((row + half) * WP, 8)
                    around = pltpu.roll(ext[pl.ds(at, WP), :], WP - col_shift, 0)
                    rows.append(around[index * WIN : (index + 1) * WIN])
            at = (step * len(cols) + index) * WIN_TOK + quarter * 16
            picked[pl.ds(pl.multiple_of(at, 16), 16), :] = jnp.concatenate(rows, axis=0).astype(BF16)

    block = total // 2 if total > 512 else total

    @pl.loop(0, 3)
    def _(n):
        weights(n).wait()
        lanes = pl.ds(pl.multiple_of(n * D, D), D)

        @pl.loop(0, total // block, unroll=total // block)
        def _(m):
            rows = pl.ds(pl.multiple_of(m * block, block), block)
            qkv[rows, lanes] = jnp.dot(
                picked[rows, :], qkv_weight[:, lanes], preferred_element_type=F32
            ).astype(BF16)

    if later is not None:
        later()
    edge_rows = first == 0
    if edge_rows:

        @pl.loop(0, WIN)
        def _(i):
            query_flag = jnp.where(i >= WIN - row_shift, 1, 0)
            key_row = (lax.broadcasted_iota(jnp.int32, (WIN, LANES), 1) % WIN_TOK) // WIN
            key_flag = jnp.where(key_row >= WIN - row_shift, 1, 0)
            bias[1, pl.ds(pl.multiple_of(i * WIN, 8), WIN), :] = jnp.where(key_flag == query_flag, 0.0, 1.0)

        bias[0] = jnp.zeros((WIN_TOK, LANES), F32)

    for step in range(count):
        row = first + stride * step
        mask = bias.at[jnp.where(row == special, 1, 0)] if row in (0, 4) else None

        @pl.loop(0, D // LANES, unroll=8)
        def _(group, step=step, mask=mask):
            for index in range(len(cols)):
                result = attention_group(qkv, mask, ones, step * len(cols) + index, group)
                lanes = pl.ds(pl.multiple_of(group * LANES, LANES), LANES)
                for i in range(WIN):
                    store(step, index, i, lanes, result[i * WIN : (i + 1) * WIN])


def attention_group(qkv, mask, ones, slot, group):
    rows = pl.ds(pl.multiple_of(slot * WIN_TOK, WIN_TOK), WIN_TOK)
    lanes = lambda part: pl.ds(pl.multiple_of(part * D + group * LANES, LANES), LANES)
    query, key, value = (qkv[rows, lanes(part)] for part in range(3))
    head_of_lane = lax.broadcasted_iota(jnp.int32, (WIN_TOK, LANES), 1) // HEAD
    zero = jnp.zeros((WIN_TOK, LANES), BF16)
    spread = lambda x: jnp.concatenate([jnp.where(head_of_lane == h, x, zero) for h in range(4)], axis=0)
    scores = lax.dot_general(query, spread(key), (((1,), (1,)), ((), ())), preferred_element_type=F32)
    low = lax.broadcasted_iota(jnp.int32, (WIN_TOK, LANES), 1) < WIN_TOK
    parts = []
    for half in range(2):
        part = scores[:, half * LANES : (half + 1) * LANES]
        if mask is not None:
            part = jnp.where(mask[...] < 0.5, part, EXCLUDED)
        low_max = jnp.max(jnp.where(low, part, -jnp.inf), axis=-1, keepdims=True)
        high_max = jnp.max(jnp.where(low, -jnp.inf, part), axis=-1, keepdims=True)
        parts.append(jnp.exp2((part - jnp.where(low, low_max, high_max)) * EXP_SCALE).astype(BF16))
    weights = jnp.concatenate(parts, axis=1)
    both = jnp.dot(weights, jnp.concatenate([spread(value), ones[...]], axis=1), preferred_element_type=F32)
    total = both[:, LANES:]
    inverse = pl.reciprocal(total, approx=True)
    inverse = inverse * (2.0 - total * inverse)
    return (both[:, :LANES] * inverse).astype(BF16).astype(F32)


def windows_kernel(windows, *refs):
    if windows is INNER:
        *refs, normed, normed_sems = refs
    meta_ref, *sources, qkv_hbm, out, ext, picked, qkv, qkv_weight, bias, ones, weight_sems = refs

    def arrival(half):
        rows = pl.ds(half * (TOKENS // 2), TOKENS // 2)
        return pltpu.make_async_copy(sources[0].at[rows], normed.at[rows], normed_sems.at[half])

    if windows is INNER:
        for half in range(2):
            arrival(half).start()

    def fill():
        if windows is INNER:
            for half in range(2):
                arrival(half).wait()
                place(normed, half * (TOKENS // 2), ext, WP, HP // 2, half * (HP // 2), 0, WP)
            return WIN
        for index, source in enumerate(sources):
            for col in range(3):
                place(source, col * WIN_TOK, ext, WP, WIN, index * WIN, col * WIN, WIN)
        return 2 * WIN

    def store(step, index, i, lanes, value):
        out[step * WIN + i, index * WIN : (index + 1) * WIN, lanes] = value

    attend(windows, meta_ref, ext, qkv_hbm, picked, qkv, qkv_weight, bias, ones, weight_sems, fill, store)


def attend_scratch(windows):
    rows = slots_of(windows) * WIN_TOK
    return [
        pltpu.VMEM((EXT_R * 4 * WIN if windows is SIDES else HP * WP, D), F32),
        pltpu.VMEM((rows, D), BF16),
        pltpu.VMEM((rows, 3 * D), BF16),
        pltpu.VMEM((D, 3 * D), BF16),
        pltpu.VMEM((2, WIN_TOK, LANES), F32),
        pltpu.VMEM((4 * WIN_TOK, LANES), BF16),
        pltpu.SemaphoreType.DMA((3,)),
    ]


def attend_windows(windows, name, meta, sources, qkv_weight):
    rows = slots_of(windows) * WIN_TOK
    return pl.pallas_call(
        lambda *refs: windows_kernel(windows, *refs),
        in_specs=[SMEM_SPEC] + [HBM_SPEC if windows is INNER else VMEM_SPEC] * len(sources) + [HBM_SPEC],
        out_specs=VMEM_SPEC,
        out_shape=jax.ShapeDtypeStruct((windows[2] * WIN, 2 * WIN, D), F32),
        scratch_shapes=attend_scratch(windows)
        + ([pltpu.VMEM((TOKENS, D), BF16), pltpu.SemaphoreType.DMA((2,))] if windows is INNER else []),
        compiler_params=pltpu.CompilerParams(vmem_limit_bytes=28 * MIB),
        cost_estimate=pl.CostEstimate(
            flops=rows * D * 3 * D * 3, bytes_accessed=12 * 10**6, transcendentals=rows * 2048
        ),
        name=name,
    )(meta, *sources, in_hbm(qkv_weight))


def tail_kernel(
    meta_ref, tiles_ref, cells_ref, tokens_hbm,
    west_ref, east_ref, from_west_ref, from_east_ref, own_west_ref, own_east_ref, west_corners_ref, east_corners_ref,
    inner_hbm, edges_hbm, out_gain_ref, read_ref, qkv_hbm, proj_hbm, unembed_hbm,
    out_ref,
    ext, picked, qkv, qkv_weight, bias, ones, weight_sems,
    mixed, mixed_rows, tokens, decoded, read_pair,
    proj_weight, unembed_weight, in_sems,
):
    row_shift, col_shift = meta_ref[0], meta_ref[1]
    inner_cols = pl.ds(WIN, 2 * WIN)
    moves = (
        (inner_hbm, mixed.at[pl.ds(WIN, 3 * WIN), inner_cols, :]),
        (edges_hbm.at[pl.ds(0, WIN)], mixed.at[pl.ds(0, WIN), inner_cols, :]),
        (edges_hbm.at[pl.ds(WIN, WIN)], mixed.at[pl.ds(SPAN_R - WIN, WIN), inner_cols, :]),
        (proj_hbm, proj_weight),
        (tokens_hbm, tokens),
        (unembed_hbm, unembed_weight),
    )
    copies = [pltpu.make_async_copy(src, dst, in_sems.at[i]) for i, (src, dst) in enumerate(moves)]

    def fill():
        columns = (
            (from_west_ref, west_corners_ref), (west_ref, own_west_ref),
            (east_ref, own_east_ref), (from_east_ref, east_corners_ref),
        )
        for index, (middle, ends) in enumerate(columns):
            place(middle, 0, ext, 4 * WIN, HP, WIN, index * WIN, WIN)
            place(ends, 0, ext, 4 * WIN, WIN, 0, index * WIN, WIN)
            place(ends, WIN_TOK, ext, 4 * WIN, WIN, WIN + HP, index * WIN, WIN)
        read_pair[...] = jnp.zeros((2 * CH, 2 * CH), BF16)
        read_pair[:CH, :CH] = read_ref[...]
        read_pair[CH:, CH:] = read_ref[...]
        return WIN

    def store(step, index, i, lanes, value):
        mixed[step * WIN + i, index * 3 * WIN : index * 3 * WIN + WIN, lanes] = value

    def later():
        for copy in copies:
            copy.start()

    attend(SIDES, meta_ref, ext, qkv_hbm, picked, qkv, qkv_weight, bias, ones, weight_sems, fill, store, later)
    for copy in copies[:5]:
        copy.wait()

    @pl.loop(0, HP // 2, unroll=2)
    def _(pair):
        rows = [
            pltpu.roll(mixed[WIN - row_shift + pair * 2 + half], SPAN_C - WIN + col_shift, 0)[:WP]
            for half in range(2)
        ]
        mixed_rows[pl.ds(pl.multiple_of(pair * 2 * WP, 2 * WP), 2 * WP), :] = jnp.concatenate(
            rows, axis=0
        ).astype(BF16)

    @pl.loop(0, TOKENS // 256, unroll=3)
    def _(m):
        rows = pl.ds(pl.multiple_of(m * 256, 256), 256)
        change = jnp.dot(mixed_rows[rows, :], proj_weight[...], preferred_element_type=F32)
        updated = (change + tokens[rows, :].astype(F32)).astype(BF16).astype(F32)
        mixed_rows[rows, :] = layer_norm(updated, out_gain_ref[...]).astype(BF16)

    copies[5].wait()

    @pl.loop(0, 2)
    def _(n):
        cols = pl.ds(pl.multiple_of(n * D, D), D)

        @pl.loop(0, 3, unroll=3)
        def _(m):
            rows = pl.ds(pl.multiple_of(m * 256, 256), 256)
            quad = jnp.dot(
                mixed_rows[rows, :], unembed_weight[:, cols], preferred_element_type=F32
            ).astype(BF16)
            for k in range(4):
                cells = jnp.dot(
                    quad[:, k * COLS : (k + 1) * COLS], read_pair[...], preferred_element_type=F32
                )
                pair = jnp.concatenate(
                    [cells[:, :CH].reshape(32, 8, CH), cells[:, CH:].reshape(32, 8, CH)], axis=1
                ).astype(BF16)
                place_at = pl.multiple_of(n * 64 + k * 16, 16)
                decoded[pl.ds(m * 32, 32), pl.ds(place_at, 16), :] = pair

    cell_iota = lax.broadcasted_iota(jnp.int32, (TILE, TILE), 0)

    @pl.loop(0, BLOCKS // GROUP, unroll=2)
    def _(part):
        for b in range(GROUP):
            block = part * GROUP + b
            cells = cells_ref[pl.ds(block, 1), :]
            one_hot = jnp.where(cell_iota == cells, 1.0, 0.0).astype(BF16)
            out_ref[block] = lax.dot_general(
                one_hot, decoded[tiles_ref[block]], (((0,), (0,)), ((), ())), preferred_element_type=F32
            ).astype(BF16)


def tail(meta, block_tiles, live_cells, tokens, sides, mixed_parts, out_gain, read_weight, qkv_weight, proj_weight, unembed_weight):
    return pl.pallas_call(
        tail_kernel,
        in_specs=[SMEM_SPEC, SMEM_SPEC] + [VMEM_SPEC, HBM_SPEC] + [VMEM_SPEC] * 8 + [HBM_SPEC] * 2 + [VMEM_SPEC] * 2 + [HBM_SPEC] * 3,
        out_specs=VMEM_SPEC,
        out_shape=pltpu.VMEM((BLOCKS, TILE, CH), BF16),
        scratch_shapes=attend_scratch(SIDES)
        + [
            pltpu.VMEM((SPAN_R, SPAN_C, D), F32),
            pltpu.VMEM((TOKENS, D), BF16),
            pltpu.VMEM((TOKENS, D), BF16),
            pltpu.VMEM((TILES, TILE, CH), BF16),
            pltpu.VMEM((2 * CH, 2 * CH), BF16),
            pltpu.VMEM((D, D), BF16),
            pltpu.VMEM((D, 2 * D), BF16),
            pltpu.SemaphoreType.DMA((6,)),
        ],
        compiler_params=pltpu.CompilerParams(vmem_limit_bytes=40 * MIB),
        cost_estimate=pl.CostEstimate(flops=12 * 10**9, bytes_accessed=28 * 10**6, transcendentals=10**6),
        name="sides_decode",
    )(
        meta, block_tiles, live_cells, in_hbm(tokens), *sides, *mixed_parts,
        out_gain, read_weight, in_hbm(qkv_weight), in_hbm(proj_weight), in_hbm(unembed_weight),
    )


def send(value, lon_step, lat_step):
    lon, lat = lax.axis_size("lon"), lax.axis_size("lat")
    pairs = [
        (i * lat + j, (i + lon_step) % lon * lat + (j + lat_step) % lat) for i in range(lon) for j in range(lat)
    ]
    return lax.ppermute(value, ("lon", "lat"), pairs)


def attention_and_decode(meta, block_tiles, live_cells, tokens, normed, west, east, north, south, out_gain, read_weight, qkv_weight, proj_weight, unembed_weight):
    from_north, from_south = send(south, 0, 1), send(north, 0, -1)
    from_west, from_east = send(east, 1, 0), send(west, -1, 0)
    inner = attend_windows(INNER, "inner_windows", meta, (in_hbm(normed),), qkv_weight)
    from_north, from_south, from_west, from_east, inner = lax.optimization_barrier(
        (from_north, from_south, from_west, from_east, inner)
    )
    first, last = slice(0, WIN_TOK), slice(2 * WIN_TOK, 3 * WIN_TOK)
    own_west = jnp.concatenate([from_north[first], from_south[first]], axis=0)
    own_east = jnp.concatenate([from_north[last], from_south[last]], axis=0)
    west_corners, east_corners = send(own_east, 1, 0), send(own_west, -1, 0)
    edges = attend_windows(EDGES, "edge_windows", meta, (from_north, north, south, from_south), qkv_weight)
    west_corners, east_corners, edges = lax.optimization_barrier((west_corners, east_corners, edges))
    sides = (west, east, from_west, from_east, own_west, own_east, west_corners, east_corners)
    return tail(
        meta, block_tiles, live_cells, tokens, sides, (inner, edges),
        out_gain, read_weight, qkv_weight, proj_weight, unembed_weight,
    )


def per_device(
    obs_values,
    obs_weights,
    block_counts,
    obs_cells,
    block_tiles,
    shift_offsets,
    embed_weight,
    patch_weight,
    norm_gain,
    qkv_weight,
    proj_weight,
    out_gain,
    unembed_weight,
    read_weight,
):
    outgoing = embed(
        block_counts.reshape(BLOCKS), obs_values.reshape(BLOCKS, TILE, CH), obs_weights.reshape(BLOCKS, TILE), embed_weight
    ).reshape(BLOCKS, 1, TILE, CH)
    received = lax.all_to_all(outgoing, ("lon", "lat"), split_axis=0, concat_axis=0, tiled=True)
    block_tiles = block_tiles.reshape(BLOCKS)
    tokens, normed, west, east, north, south, live_cells = grid_tokens(
        block_tiles, obs_cells.reshape(BLOCKS, TILE), norm_gain.reshape(1, D),
        received.reshape(BLOCKS, TILE, CH), patch_weight,
    )
    lat_index = lax.axis_index("lat")
    last = lax.axis_size("lat") - 1
    special = jnp.where(lat_index == 0, 0, jnp.where(lat_index == last, 4, -1)).astype(jnp.int32)
    meta = jnp.concatenate([shift_offsets, special.reshape(1)])
    sampled = attention_and_decode(
        meta, block_tiles, live_cells, tokens, normed, west, east, north, south,
        out_gain.reshape(1, D), read_weight, qkv_weight, proj_weight, unembed_weight,
    )
    returned = lax.all_to_all(
        sampled.reshape(BLOCKS, 1, TILE, CH), ("lon", "lat"), split_axis=0, concat_axis=0, tiled=True
    )
    return returned


def solution(mesh):
    rows = ("lon", "lat")
    in_specs = (
        P(rows, None, None, None),
        P(rows, None, None),
        P(rows, None),
        P(rows, None, None),
        P(rows, None),
    ) + (P(),) * 9
    out_specs = P(rows, None, None, None)
    return jax.shard_map(
        per_device, mesh=mesh, in_specs=in_specs, out_specs=out_specs, check_vma=False
    )
```
